32 devices in a mesh: group: 4 (over y, x), mp: 8 (over z, core).
Axes of the slice: x: 2, y: 2, z: 4, core: 2. Of those that a mesh axis runs over, the one named last changes fastest.
Arguments:
- inputs: bfloat16 [2, 3072, 8192], P(None, 'group', 'mp'), may hold values from -6 to 6
- targets: bfloat16 [2, 3072, 1024], P(None, ('group', 'mp')), may hold values from -6 to 6
- numerator: bfloat16 [4, 8192, 1024], P('group', 'mp'), may hold values from -6 to 6
- momentum: float32 [4, 8192, 1024], P('group', 'mp'), may hold values from -4 to 4
- received: bfloat16 [4, 8192, 1024], P('group', 'mp'), may hold values from -6 to 6
- push_weight: float32 [4], P('group'), may hold values from 0.5 to 2
- received_weight: float32 [4], P('group'), may hold values from 0.5 to 2
- mix_share: int32 [4, 2], P('group'), may hold values from 1 to 7
Outputs:
- final_numerator: bfloat16 [4, 8192, 1024], P('group', 'mp')
- final_weight: float32 [4], P('group')
- final_received: bfloat16 [4, 8192, 1024], P('group', 'mp')
- final_received_weight: float32 [4], P('group')
- value_rows: bfloat16 [2, 3072, 1024], P(None, ('group', 'mp'))
The draws below stay inside these ranges and needn't reach their ends.
All inputs are finite; a program needn't handle non-finite values.
Results may differ from the reference program's by a relative error of at most 0.02.
Values may be sent and summed in bfloat16 or wider, within the bound.
A program may use at most 64 MiB of HBM per device.

```python
import math
import jax
import jax.numpy as jnp
from jax import lax

D = 8192
KV = 1024
TOK_GRP = 768
STEPS = 2
TOKENS = 3072
N_GROUP = 4
N_MP = 8


def place_ends(values, stream_key, smallest, high):
    spot = [jax.random.randint(jax.random.fold_in(stream_key, axis), (), 0, length) for axis, length in enumerate(values.shape)]
    widest = values.shape.index(max(values.shape))
    neighbour = spot[:widest] + [(spot[widest] + 1) % values.shape[widest]] + spot[widest + 1:]
    return values.at[tuple(spot)].set(smallest).at[tuple(neighbour)].set(high)


def block_levels(stream_key, dims, shards, low, high):
    loudness, own = 1.0, jax.random.fold_in(stream_key, 6)
    for dim, parts in shards:
        heights = jnp.exp(jax.random.uniform(jax.random.fold_in(own, dim), (parts,), jnp.float32, low / len(shards), high / len(shards)))
        loudness = loudness * jnp.repeat(heights, dims[dim] // parts).reshape([-1 if axis == dim else 1 for axis in range(len(dims))])
    return loudness


def centred(key, dims, scale, bound, split=(), held_as=jnp.bfloat16):
    gain = block_levels(key, dims, split, -0.22, 0.18) if split else 1.0
    values = jax.random.normal(key, dims, jnp.float32) * scale * gain
    return jnp.minimum(jnp.maximum(values, -bound), bound).astype(held_as)


def setup_inputs(seed: int = 0) -> dict:
    seeds = jax.random.split(jax.random.key(seed), 9)
    return {
        "inputs": centred(seeds[0], (STEPS, TOKENS, D), 1.0, 6.0, ((1, 4), (2, 8))),
        "targets": centred(seeds[1], (STEPS, TOKENS, KV), 1.0, 6.0, ((1, 32),)),
        "numerator": centred(seeds[2], (N_GROUP, D, KV), 1.0, 6.0, ((0, 4), (1, 8))),
        "momentum": centred(seeds[3], (N_GROUP, D, KV), 0.5, 4.0, ((0, 4), (1, 8)), jnp.float32),
        "received": centred(seeds[4], (N_GROUP, D, KV), 1.0, 6.0, ((0, 4), (1, 8))),
        "push_weight": jnp.clip(jnp.exp(math.log(2.0) - 1.3862944 * jax.random.uniform(seeds[5], (N_GROUP,), jnp.float32) ** block_levels(seeds[5], (N_GROUP,), ((0, 4),), -0.2, 0.2)), 0.5, 2.0),
        "received_weight": jnp.clip(jnp.exp(math.log(2.0) - 1.3862944 * jax.random.uniform(seeds[6], (N_GROUP,), jnp.float32) ** block_levels(seeds[6], (N_GROUP,), ((0, 4),), -0.2, 0.2)), 0.5, 2.0),
        "mix_share": place_ends(jax.random.randint(seeds[7], (N_GROUP, STEPS), 1, 8), jax.random.fold_in(seeds[7], 1), 1, 7).astype(jnp.int32),
    }


momentum_decay = 0.9
step_size = 0.5

def reference(inputs, targets, numerator, momentum, received, push_weight, received_weight, mix_share):
    block_width = D // N_MP
    row_scale = 1.0 / math.sqrt(D)
    grad_scale = 1.0 / math.sqrt(TOK_GRP)
    current = numerator
    velocity = momentum
    arrived = received
    arrived_weight = received_weight
    weights = push_weight
    value_steps = []
    for step_index in range(STEPS):
        hop_length = 2 ** step_index
        new_current, new_velocity, outgoing_all, outgoing_weights, new_weights, group_values = ([], [], [], [], [], [])
        for group_index in range(N_GROUP):
            group_weight = weights[group_index]
            scaled = (current[group_index].astype(jnp.float32) / group_weight).astype(jnp.bfloat16)
            group_tokens = inputs[step_index, group_index * TOK_GRP:(group_index + 1) * TOK_GRP]
            partials = jnp.einsum('tkd,kdo->kto', group_tokens.reshape(TOK_GRP, N_MP, block_width).astype(jnp.float32), scaled.reshape(N_MP, block_width, KV).astype(jnp.float32)) * row_scale
            partials = lax.optimization_barrier(partials.astype(jnp.bfloat16)).astype(jnp.float32)
            values = lax.optimization_barrier(jnp.sum(partials, axis=0)).astype(jnp.bfloat16)
            teacher = targets[step_index, group_index * TOK_GRP:(group_index + 1) * TOK_GRP]
            residual = (values.astype(jnp.float32) - teacher.astype(jnp.float32)).astype(jnp.bfloat16)
            gradient = jnp.dot(group_tokens.T, residual, preferred_element_type=jnp.float32) * grad_scale
            moved = momentum_decay * velocity[group_index] + gradient
            half_step = current[group_index].astype(jnp.float32) - step_size * moved
            kept_share = mix_share[group_index, step_index].astype(jnp.float32) / 8.0
            outgoing_all.append(((1.0 - kept_share) * half_step).astype(jnp.bfloat16))
            outgoing_weights.append(((1.0 - kept_share) * group_weight).astype(jnp.bfloat16).astype(jnp.float32))
            new_current.append((kept_share * half_step + arrived[group_index].astype(jnp.float32)).astype(jnp.bfloat16))
            new_weights.append(kept_share * group_weight + arrived_weight[group_index])
            new_velocity.append(moved)
            group_values.append(values)
        current = jnp.stack(new_current)
        velocity = jnp.stack(new_velocity)
        weights = jnp.stack(new_weights)
        arrived = jnp.roll(jnp.stack(outgoing_all), hop_length, axis=0)
        arrived_weight = jnp.roll(jnp.stack(outgoing_weights), hop_length, axis=0)
        value_steps.append(jnp.concatenate(group_values, axis=0))
    return (current, weights, arrived, arrived_weight, jnp.stack(value_steps))
```

```python
import functools
import math

import jax
import jax.numpy as jnp
from jax import lax
from jax.experimental import pallas as pl
from jax.experimental.pallas import tpu as pltpu
from jax.sharding import PartitionSpec as P

D = 8192
TOK_GRP = 768

momentum_decay = 0.9
step_size = 0.5
MESH = pl.DeviceIdType.MESH
f32, bf16 = jnp.float32, jnp.bfloat16


def kernel(
    n_group, n_mp, chunks, steps,
    pw_ref, rw_ref, mix_ref, x_hbm, tgt_hbm, num_hbm, mom_hbm, rec_hbm,
    fnum_hbm, frec_hbm, vr_hbm, fw_ref, frw_ref,
    x, xt, cur, vel, arr, tgt, part, sib, pair, peers, res, out, sc, val, wsend, wrecv,
    load_sem, sib_send, sib_recv, rs_send, rs_recv, ag_send, ag_recv, fwd_send, fwd_recv,
    msg_send, msg_recv, w_send, w_recv, store_sem,
):
    row_scale = 1.0 / math.sqrt(D)
    grad_scale = 1.0 / math.sqrt(TOK_GRP)
    nz = n_mp // 2
    rows, width = x.shape[1], x.shape[2]
    own = rows // n_mp
    cols = cur.shape[2]
    jobs = steps * chunks
    g = lax.axis_index("group")
    m = lax.axis_index("mp")
    z = m // 2
    core = m % 2
    other = 1 - core
    sibling = z * 2 + other

    def z_peer(d):
        return lax.rem(z + d, nz) * 2 + core

    def g_peer(d):
        return lax.rem(g + d + n_group, n_group)

    def span(c):
        return pl.ds(c * cols, cols)

    loads = {}

    def load(name, src, dst):
        copy = pltpu.make_async_copy(src, dst, load_sem.at[len(loads)])
        copy.start()
        loads[name] = copy

    load("num0", num_hbm.at[0, :, span(0)], cur.at[0])
    load("x0", x_hbm.at[0], x.at[0])
    for c in range(1, chunks):
        load(f"num{c}", num_hbm.at[0, :, span(c)], cur.at[c])
    for c in range(chunks):
        for s in range(steps):
            load(f"tgt{s}_{c}", tgt_hbm.at[s, :, span(c)], tgt.at[s * chunks + c])
    for c in range(chunks):
        load(f"mom{c}", mom_hbm.at[0, :, span(c)], vel.at[c])
        load(f"rec{c}", rec_hbm.at[0, :, span(c)], arr.at[c])
    for s in range(1, steps):
        load(f"x{s}", x_hbm.at[s], x.at[s])

    barrier = pltpu.get_barrier_semaphore()
    offsets = []
    for s in range(steps):
        for d in (2**s, -(2**s)):
            if d % n_group and d % n_group not in offsets:
                offsets.append(d % n_group)
    for d in offsets:
        pl.semaphore_signal(barrier, inc=1, device_id={"group": g_peer(d)}, device_id_type=MESH)
    for d in range(1, nz):
        pl.semaphore_signal(barrier, inc=1, device_id={"mp": z_peer(d)}, device_id_type=MESH)
    pl.semaphore_signal(barrier, inc=1, device_id={"mp": sibling}, device_id_type=MESH)
    pl.semaphore_wait(barrier, len(offsets) + nz)

    keep = [mix_ref[0, s].astype(f32) / 8.0 for s in range(steps)]
    weights = [pw_ref[0], keep[0] * pw_ref[0] + rw_ref[0]]
    w_copies = []
    for s in range(steps):
        outgoing_weight = jnp.full(wsend.shape[1:], (1.0 - keep[s]) * weights[s], f32)
        wsend[s] = outgoing_weight.astype(bf16).astype(f32)
        copy = pltpu.make_async_remote_copy(
            wsend.at[s], wrecv.at[s], w_send.at[s], w_recv.at[s],
            device_id={"group": g_peer(2**s)}, device_id_type=MESH,
        )
        copy.start()
        w_copies.append(copy)

    sends, stores = [], []
    sib_c, rs_c, ag_c, fwd_c, msg_c = {}, {}, {}, {}, {}

    def remote(src, dst, send, recv, where):
        copy = pltpu.make_async_remote_copy(src, dst, send, recv, device_id=where, device_id_type=MESH)
        copy.start()
        sends.append(copy)
        return copy

    def forward(j):
        s, c = divmod(j, chunks)
        if s == 0:
            loads[f"num{c}"].wait()
        if j == 0:
            loads["x0"].wait()
        sc[...] = (cur[c].astype(f32) / weights[s]).astype(bf16)
        half_z = nz // 2
        tile = half_z * 2 * own

        def body(i, _):
            lhs = x[s, pl.ds(pl.multiple_of(i * tile, tile), tile), :]
            product = jnp.dot(lhs, sc[...], preferred_element_type=f32) * row_scale
            part[j, pl.ds(i * half_z, half_z)] = product.astype(bf16).reshape(half_z, 2, own, cols)
            return 0

        lax.fori_loop(0, 2, body, 0)
        sib_c[j] = remote(part.at[j, :, other], sib.at[j], sib_send.at[j], sib_recv.at[j], {"mp": sibling})

    def pair_sum(j):
        sib_c[j].wait_recv()
        for k in range(nz):
            pair[j, k] = (part[j, k, core].astype(f32) + sib[j, k].astype(f32)).astype(bf16)
        for d in range(1, nz):
            rs_c[j, d] = remote(
                pair.at[j, lax.rem(z + d, nz)], peers.at[j, d - 1],
                rs_send.at[j, d - 1], rs_recv.at[j, d - 1], {"mp": z_peer(d)},
            )

    def value(j):
        s, c = divmod(j, chunks)
        total = pair[j, z].astype(f32)
        for d in range(1, nz):
            rs_c[j, d].wait_recv()
            total += peers[j, d - 1].astype(f32)
        values = total.astype(bf16)
        val[j] = values
        loads[f"tgt{s}_{c}"].wait()
        res[j, z, core] = (values.astype(f32) - tgt[j].astype(f32)).astype(bf16)
        for d in range(1, nz):
            ag_c[j, d] = remote(
                res.at[j, z, core], res.at[j, z, core],
                ag_send.at[j, d - 1], ag_recv.at[j, d - 1], {"mp": z_peer(d)},
            )
        store = pltpu.make_async_copy(val.at[j], vr_hbm.at[s, :, span(c)], store_sem.at[j])
        store.start()
        stores.append(store)

    def pass_on(j):
        for d in range(1, nz):
            source = lax.rem(z - d + nz, nz)
            pltpu.make_async_remote_copy(
                res.at[j, z, core], res.at[j, source, core],
                ag_send.at[j, d - 1], ag_recv.at[j, d - 1],
                device_id={"mp": z_peer(d)}, device_id_type=MESH,
            ).wait_recv()
        remote(res.at[j, :, core], res.at[j, :, core], fwd_send.at[j], fwd_recv.at[j], {"mp": sibling})

    def update(j):
        s, c = divmod(j, chunks)
        pltpu.make_async_remote_copy(
            res.at[j, :, core], res.at[j, :, other], fwd_send.at[j], fwd_recv.at[j],
            device_id={"mp": sibling}, device_id_type=MESH,
        ).wait_recv()
        if s == 0:
            loads[f"mom{c}"].wait()
            loads[f"rec{c}"].wait()
        else:
            msg_c[j - chunks].wait_recv()
        tile = min(256, width)

        def body(i, _):
            at = pl.ds(pl.multiple_of(i * tile, tile), tile)
            gradient = jnp.dot(
                xt[s, at, :], res[j].reshape(rows, cols), preferred_element_type=f32
            ) * grad_scale
            velocity = momentum_decay * vel[c, at, :] + gradient
            vel[c, at, :] = velocity
            half_step = cur[c, at, :].astype(f32) - step_size * velocity
            out[j, at, :] = ((1.0 - keep[s]) * half_step).astype(bf16)
            landed = arr[c, at, :] if s == 0 else arr[chunks + c, at, :]
            cur[c, at, :] = (keep[s] * half_step + landed.astype(f32)).astype(bf16)
            return 0

        lax.fori_loop(0, width // tile, body, 0)
        target = arr.at[chunks + c] if s == 0 else frec_hbm.at[0, :, span(c)]
        msg_c[j] = remote(out.at[j], target, msg_send.at[j], msg_recv.at[j], {"group": g_peer(2**s)})
        if s == steps - 1:
            store = pltpu.make_async_copy(cur.at[c], fnum_hbm.at[0, :, span(c)], store_sem.at[jobs + c])
            store.start()
            stores.append(store)

    def transpose(s):
        if s > 0:
            loads[f"x{s}"].wait()
        tile = min(256, width)
        for i in range(width // tile):
            xt[s, i * tile:(i + 1) * tile, :] = x[s, :, i * tile:(i + 1) * tile].T

    stages = (forward, pair_sum, value, pass_on, update)
    for tick in range(jobs + len(stages) - 1):
        for k in reversed(range(len(stages))):
            j = tick - k
            if 0 <= j < jobs:
                stages[k](j)
        if tick == 0:
            transpose(0)
        if tick == 2:
            for s in range(1, steps):
                transpose(s)

    for copy in w_copies:
        copy.wait()
    fw_ref[...] = keep[1] * weights[1] + wrecv[0]
    frw_ref[...] = wrecv[1]
    for c in range(chunks):
        msg_c[(steps - 1) * chunks + c].wait_recv()
    for copy in sends:
        copy.wait_send()
    for store in stores:
        store.wait()


def local(inputs, targets, numerator, momentum, received, push_weight, received_weight, mix_share):
    steps, rows, width = inputs.shape
    own, kv = targets.shape[1], targets.shape[2]
    n_group, n_mp = lax.axis_size("group"), lax.axis_size("mp")
    chunks = 4
    cols = kv // chunks
    jobs = steps * chunks
    nz = n_mp // 2
    any_space = pl.BlockSpec(memory_space=pl.ANY)
    smem = pl.BlockSpec(memory_space=pltpu.SMEM)
    vmem = pl.BlockSpec(memory_space=pltpu.VMEM)
    dma = pltpu.SemaphoreType.DMA
    fnum, frec, vr, fw, frw = pl.pallas_call(
        functools.partial(kernel, n_group, n_mp, chunks, steps),
        out_shape=(
            jax.ShapeDtypeStruct(numerator.shape, bf16),
            jax.ShapeDtypeStruct(numerator.shape, bf16),
            jax.ShapeDtypeStruct(targets.shape, bf16),
            jax.ShapeDtypeStruct((8, 128), f32),
            jax.ShapeDtypeStruct((8, 128), f32),
        ),
        in_specs=[smem] * 3 + [any_space] * 5,
        out_specs=(any_space, any_space, any_space, vmem, vmem),
        scratch_shapes=[
            pltpu.VMEM((steps, rows, width), bf16),
            pltpu.VMEM((steps, width, rows), bf16),
            pltpu.VMEM((chunks, width, cols), bf16),
            pltpu.VMEM((chunks, width, cols), f32),
            pltpu.VMEM((2 * chunks, width, cols), bf16),
            pltpu.VMEM((jobs, own, cols), bf16),
            pltpu.VMEM((jobs, nz, 2, own, cols), bf16),
            pltpu.VMEM((jobs, nz, own, cols), bf16),
            pltpu.VMEM((jobs, nz, own, cols), bf16),
            pltpu.VMEM((jobs, nz - 1, own, cols), bf16),
            pltpu.VMEM((jobs, nz, 2, own, cols), bf16),
            pltpu.VMEM((jobs, width, cols), bf16),
            pltpu.VMEM((width, cols), bf16),
            pltpu.VMEM((jobs, own, cols), bf16),
            pltpu.VMEM((steps, 8, 128), f32),
            pltpu.VMEM((steps, 8, 128), f32),
            dma((3 * chunks + steps * chunks + steps,)),
            dma((jobs,)), dma((jobs,)),
            dma((jobs, nz - 1)), dma((jobs, nz - 1)),
            dma((jobs, nz - 1)), dma((jobs, nz - 1)),
            dma((jobs,)), dma((jobs,)),
            dma((jobs,)), dma((jobs,)),
            dma((steps,)), dma((steps,)),
            dma((jobs + chunks,)),
        ],
        compiler_params=pltpu.CompilerParams(
            collective_id=0, has_side_effects=True, vmem_limit_bytes=58 * 1024 * 1024
        ),
    )(push_weight, received_weight, mix_share, inputs, targets, numerator, momentum, received)
    return fnum, fw[0, :1], frec, frw[0, :1], vr


def solution(mesh):
    placed = (
        P(None, "group", "mp"),
        P(None, ("group", "mp"), None),
        P("group", "mp", None),
        P("group", "mp", None),
        P("group", "mp", None),
        P("group"),
        P("group"),
        P("group", None),
    )
    return jax.shard_map(
        local,
        mesh=mesh,
        in_specs=placed,
        out_specs=(
            P("group", "mp", None),
            P("group"),
            P("group", "mp", None),
            P("group"),
            P(None, ("group", "mp"), None),
        ),
        check_vma=False,
    )
```

```python
import functools
import math

import jax
import jax.numpy as jnp
from jax import lax
from jax.experimental import pallas as pl
from jax.experimental.pallas import tpu as pltpu
from jax.sharding import PartitionSpec as P

D = 8192
TOK_GRP = 768

momentum_decay = 0.9
step_size = 0.5
MESH = pl.DeviceIdType.MESH
f32, bf16 = jnp.float32, jnp.bfloat16


def kernel(
    n_group, n_mp, chunks, steps,
    pw_ref, rw_ref, mix_ref, x_hbm, tgt_hbm, num_hbm, mom_hbm, rec_hbm,
    fnum_hbm, frec_hbm, vr_hbm, fw_ref, frw_ref,
    x, xt, cur, vel, arr, tgt, part, sib, pair, peers, res, out, sc, val, wsend, wrecv,
    load_sem, sib_send, sib_recv, rs_send, rs_recv, ag_send, ag_recv, fwd_send, fwd_recv,
    msg_send, msg_recv, relay_send, w_send, w_recv, store_sem,
):
    row_scale = 1.0 / math.sqrt(D)
    grad_scale = 1.0 / math.sqrt(TOK_GRP)
    nz = n_mp // 2
    rows, width = x.shape[1], x.shape[2]
    own = rows // n_mp
    cols = cur.shape[2]
    jobs = steps * chunks
    g = lax.axis_index("group")
    m = lax.axis_index("mp")
    z = m // 2
    core = m % 2
    other = 1 - core
    odd = g % 2

    def relayed(c):
        return n_group % 2 == 0 and n_group > 2 and c % 2 == 1

    sibling = z * 2 + other

    def z_peer(d):
        return lax.rem(z + d, nz) * 2 + core

    def g_peer(d):
        return lax.rem(g + d + n_group, n_group)

    def span(c):
        return pl.ds(c * cols, cols)

    loads = {}

    def load(name, src, dst):
        copy = pltpu.make_async_copy(src, dst, load_sem.at[len(loads)])
        copy.start()
        loads[name] = copy

    load("num0", num_hbm.at[0, :, span(0)], cur.at[0])
    load("x0", x_hbm.at[0], x.at[0])
    for c in range(1, chunks):
        load(f"num{c}", num_hbm.at[0, :, span(c)], cur.at[c])
    for s in range(steps):
        load(f"tgt{s}", tgt_hbm.at[s], tgt.at[s])
    for c in range(chunks):
        load(f"mom{c}", mom_hbm.at[0, :, span(c)], vel.at[c])
        load(f"rec{c}", rec_hbm.at[0, :, span(c)], arr.at[c])
    for s in range(1, steps):
        load(f"x{s}", x_hbm.at[s], x.at[s])

    barrier = pltpu.get_barrier_semaphore()
    offsets = []
    for s in range(steps):
        for d in (2**s, -(2**s)):
            if d % n_group and d % n_group not in offsets:
                offsets.append(d % n_group)
    for d in offsets:
        pl.semaphore_signal(barrier, inc=1, device_id={"group": g_peer(d)}, device_id_type=MESH)
    for d in range(1, nz):
        pl.semaphore_signal(barrier, inc=1, device_id={"mp": z_peer(d)}, device_id_type=MESH)
    pl.semaphore_signal(barrier, inc=1, device_id={"mp": sibling}, device_id_type=MESH)
    pl.semaphore_wait(barrier, len(offsets) + nz)

    keep = [mix_ref[0, s].astype(f32) / 8.0 for s in range(steps)]
    weights = [pw_ref[0], keep[0] * pw_ref[0] + rw_ref[0]]
    w_copies = []
    for s in range(steps):
        outgoing_weight = jnp.full(wsend.shape[1:], (1.0 - keep[s]) * weights[s], f32)
        wsend[s] = outgoing_weight.astype(bf16).astype(f32)
        copy = pltpu.make_async_remote_copy(
            wsend.at[s], wrecv.at[s], w_send.at[s], w_recv.at[s],
            device_id={"group": g_peer(2**s)}, device_id_type=MESH,
        )
        copy.start()
        w_copies.append(copy)

    sends, stores = [], []
    sib_c, rs_c, ag_c, fwd_c, msg_c = {}, {}, {}, {}, {}

    def remote(src, dst, send, recv, where):
        copy = pltpu.make_async_remote_copy(src, dst, send, recv, device_id=where, device_id_type=MESH)
        copy.start()
        sends.append(copy)
        return copy

    def forward(j):
        s, c = divmod(j, chunks)
        if s == 0:
            loads[f"num{c}"].wait()
        if j == 0:
            loads["x0"].wait()
        sc[...] = (cur[c].astype(f32) / weights[s]).astype(bf16)
        half_z = nz // 2
        tile = half_z * 2 * own

        def body(i, _):
            lhs = x[s, pl.ds(pl.multiple_of(i * tile, tile), tile), :]
            product = jnp.dot(lhs, sc[...], preferred_element_type=f32) * row_scale
            part[j, pl.ds(i * half_z, half_z)] = product.astype(bf16).reshape(half_z, 2, own, cols)
            return 0

        lax.fori_loop(0, 2, body, 0)
        sib_c[j] = remote(part.at[j, :, other], sib.at[j], sib_send.at[j], sib_recv.at[j], {"mp": sibling})

    def pair_sum(j):
        sib_c[j].wait_recv()
        for k in range(nz):
            pair[j, k] = (part[j, k, core].astype(f32) + sib[j, k].astype(f32)).astype(bf16)
        for d in range(1, nz):
            rs_c[j, d] = remote(
                pair.at[j, lax.rem(z + d, nz)], peers.at[j, d - 1],
                rs_send.at[j, d - 1], rs_recv.at[j, d - 1], {"mp": z_peer(d)},
            )

    def value(j):
        s, c = divmod(j, chunks)
        total = pair[j, z].astype(f32)
        for d in range(1, nz):
            rs_c[j, d].wait_recv()
            total += peers[j, d - 1].astype(f32)
        values = total.astype(bf16)
        columns = slice(c * cols, (c + 1) * cols)
        val[s, :, columns] = values
        if c == 0:
            loads[f"tgt{s}"].wait()
        res[j, z, core] = (values.astype(f32) - tgt[s, :, columns].astype(f32)).astype(bf16)
        for d in range(1, nz):
            ag_c[j, d] = remote(
                res.at[j, z, core], res.at[j, z, core],
                ag_send.at[j, d - 1], ag_recv.at[j, d - 1], {"mp": z_peer(d)},
            )
        if c == chunks - 1:
            store = pltpu.make_async_copy(val.at[s], vr_hbm.at[s], store_sem.at[s])
            store.start()
            stores.append(store)

    def pass_on(j):
        for d in range(1, nz):
            source = lax.rem(z - d + nz, nz)
            pltpu.make_async_remote_copy(
                res.at[j, z, core], res.at[j, source, core],
                ag_send.at[j, d - 1], ag_recv.at[j, d - 1],
                device_id={"mp": z_peer(d)}, device_id_type=MESH,
            ).wait_recv()
        remote(res.at[j, :, core], res.at[j, :, core], fwd_send.at[j], fwd_recv.at[j], {"mp": sibling})

    def update(j):
        s, c = divmod(j, chunks)
        pltpu.make_async_remote_copy(
            res.at[j, :, core], res.at[j, :, other], fwd_send.at[j], fwd_recv.at[j],
            device_id={"mp": sibling}, device_id_type=MESH,
        ).wait_recv()
        if s == 0:
            loads[f"mom{c}"].wait()
            loads[f"rec{c}"].wait()
        else:
            landing(j - chunks).wait_recv()
        tile = min(256, width)

        def body(i, _):
            at = pl.ds(pl.multiple_of(i * tile, tile), tile)
            gradient = jnp.dot(
                xt[s, at, :], res[j].reshape(rows, cols), preferred_element_type=f32
            ) * grad_scale
            velocity = momentum_decay * vel[c, at, :] + gradient
            vel[c, at, :] = velocity
            half_step = cur[c, at, :].astype(f32) - step_size * velocity
            out[j, at, :] = ((1.0 - keep[s]) * half_step).astype(bf16)
            landed = arr[c, at, :] if s == 0 else arr[chunks + c, at, :]
            cur[c, at, :] = (keep[s] * half_step + landed.astype(f32)).astype(bf16)
            return 0

        lax.fori_loop(0, width // tile, body, 0)
        if s == 0 and relayed(c):
            msg_c[j] = remote(
                out.at[j], arr.at[chunks + c + odd * chunks], msg_send.at[j],
                msg_recv.at[j + odd * jobs], {"group": g_peer(1 + odd)},
            )
        else:
            msg_c[j] = remote(
                out.at[j], arr.at[chunks + c if s == 0 else 3 * chunks + c],
                msg_send.at[j], msg_recv.at[j], {"group": g_peer(2**s)},
            )
        if s == steps - 1:
            store = pltpu.make_async_copy(cur.at[c], fnum_hbm.at[0, :, span(c)], store_sem.at[steps + c])
            store.start()
            stores.append(store)

    def landing(j):
        s, c = divmod(j, chunks)
        return pltpu.make_async_remote_copy(
            out.at[j], arr.at[chunks + c if s == 0 else 3 * chunks + c],
            msg_send.at[j], msg_recv.at[j],
            device_id={"group": g_peer(2**s)}, device_id_type=MESH,
        )

    def relay_copy(c):
        return pltpu.make_async_remote_copy(
            arr.at[2 * chunks + c], arr.at[chunks + c], relay_send.at[c], msg_recv.at[c],
            device_id={"group": g_peer(-1)}, device_id_type=MESH,
        )

    def relay(c):
        @pl.when(odd == 1)
        def _():
            pltpu.make_async_remote_copy(
                out.at[c], arr.at[2 * chunks + c], msg_send.at[c], msg_recv.at[c + jobs],
                device_id={"group": g_peer(2)}, device_id_type=MESH,
            ).wait_recv()
            relay_copy(c).start()

    def transpose(s, i, pieces):
        if s > 0 and i == 0:
            loads[f"x{s}"].wait()
        tile = width // pieces
        xt[s, i * tile:(i + 1) * tile, :] = x[s, :, i * tile:(i + 1) * tile].T

    relay_tick = 7
    stages = (forward, pair_sum, value, pass_on, update)
    for tick in range(jobs + len(stages) - 1):
        for k in reversed(range(len(stages))):
            j = tick - k
            if 0 <= j < jobs:
                stages[k](j)
        if 0 <= tick - relay_tick < chunks and relayed(tick - relay_tick):
            relay(tick - relay_tick)
        for s in range(steps):
            if 0 <= tick - s * chunks // 2 < 4:
                transpose(s, tick - s * chunks // 2, 4)

    for copy in w_copies:
        copy.wait()
    fw_ref[...] = keep[1] * weights[1] + wrecv[0]
    frw_ref[...] = wrecv[1]
    for c in range(chunks):
        landing((steps - 1) * chunks + c).wait_recv()
        store = pltpu.make_async_copy(
            arr.at[3 * chunks + c], frec_hbm.at[0, :, span(c)], store_sem.at[steps + chunks + c]
        )
        store.start()
        stores.append(store)
    for copy in sends:
        copy.wait_send()
    for c in range(chunks):
        if relayed(c):
            @pl.when(odd == 1)
            def _():
                relay_copy(c).wait_send()
    for store in stores:
        store.wait()


def finish(fnum, frec, vr, fw, frw, fnum_out, fw_out, frec_out, frw_out, vr_out, sem):
    copies = []
    for i, (src, dst) in enumerate(((fnum, fnum_out), (frec, frec_out), (vr, vr_out))):
        copies.append(pltpu.make_async_copy(src, dst, sem.at[i]))
        copies[-1].start()
    fw_out[0] = fw[0, 0]
    frw_out[0] = frw[0, 0]
    for copy in copies:
        copy.wait()


def local(inputs, targets, numerator, momentum, received, push_weight, received_weight, mix_share):
    steps, rows, width = inputs.shape
    own, kv = targets.shape[1], targets.shape[2]
    n_group, n_mp = lax.axis_size("group"), lax.axis_size("mp")
    chunks = 8
    cols = kv // chunks
    jobs = steps * chunks
    nz = n_mp // 2
    any_space = pl.BlockSpec(memory_space=pl.ANY)
    smem = pl.BlockSpec(memory_space=pltpu.SMEM)
    vmem = pl.BlockSpec(memory_space=pltpu.VMEM)
    dma = pltpu.SemaphoreType.DMA
    fnum, frec, vr, fw, frw = pl.pallas_call(
        functools.partial(kernel, n_group, n_mp, chunks, steps),
        out_shape=(
            jax.ShapeDtypeStruct(numerator.shape, bf16),
            jax.ShapeDtypeStruct(numerator.shape, bf16),
            jax.ShapeDtypeStruct(targets.shape, bf16),
            jax.ShapeDtypeStruct((8, 128), f32),
            jax.ShapeDtypeStruct((8, 128), f32),
        ),
        in_specs=[smem] * 3 + [any_space] * 5,
        out_specs=(any_space, any_space, any_space, vmem, vmem),
        scratch_shapes=[
            pltpu.VMEM((steps, rows, width), bf16),
            pltpu.VMEM((steps, width, rows), bf16),
            pltpu.VMEM((chunks, width, cols), bf16),
            pltpu.VMEM((chunks, width, cols), f32),
            pltpu.VMEM((4 * chunks, width, cols), bf16),
            pltpu.VMEM((steps, own, kv), bf16),
            pltpu.VMEM((jobs, nz, 2, own, cols), bf16),
            pltpu.VMEM((jobs, nz, own, cols), bf16),
            pltpu.VMEM((jobs, nz, own, cols), bf16),
            pltpu.VMEM((jobs, nz - 1, own, cols), bf16),
            pltpu.VMEM((jobs, nz, 2, own, cols), bf16),
            pltpu.VMEM((jobs, width, cols), bf16),
            pltpu.VMEM((width, cols), bf16),
            pltpu.VMEM((steps, own, kv), bf16),
            pltpu.VMEM((steps, 8, 128), f32),
            pltpu.VMEM((steps, 8, 128), f32),
            dma((3 * chunks + 2 * steps,)),
            dma((jobs,)), dma((jobs,)),
            dma((jobs, nz - 1)), dma((jobs, nz - 1)),
            dma((jobs, nz - 1)), dma((jobs, nz - 1)),
            dma((jobs,)), dma((jobs,)),
            dma((jobs,)), dma((2 * jobs,)), dma((chunks,)),
            dma((steps,)), dma((steps,)),
            dma((steps + 2 * chunks,)),
        ],
        compiler_params=pltpu.CompilerParams(
            collective_id=0, has_side_effects=True, vmem_limit_bytes=58 * 1024 * 1024
        ),
    )(push_weight, received_weight, mix_share, inputs, targets, numerator, momentum, received)
    return pl.pallas_call(
        finish,
        out_shape=(
            jax.ShapeDtypeStruct(numerator.shape, bf16),
            jax.ShapeDtypeStruct(push_weight.shape, f32),
            jax.ShapeDtypeStruct(numerator.shape, bf16),
            jax.ShapeDtypeStruct(push_weight.shape, f32),
            jax.ShapeDtypeStruct(targets.shape, bf16),
        ),
        in_specs=[any_space, any_space, any_space, vmem, vmem],
        out_specs=(any_space, smem, any_space, smem, any_space),
        scratch_shapes=[dma((3,))],
    )(fnum, frec, vr, fw, frw)


def solution(mesh):
    placed = (
        P(None, "group", "mp"),
        P(None, ("group", "mp"), None),
        P("group", "mp", None),
        P("group", "mp", None),
        P("group", "mp", None),
        P("group"),
        P("group"),
        P("group", None),
    )
    return jax.shard_map(
        local,
        mesh=mesh,
        in_specs=placed,
        out_specs=(
            P("group", "mp", None),
            P("group"),
            P("group", "mp", None),
            P("group"),
            P(None, ("group", "mp"), None),
        ),
        check_vma=False,
    )
```

```python
import functools
import math

import jax
import jax.numpy as jnp
from jax import lax
from jax.experimental import pallas as pl
from jax.experimental.pallas import tpu as pltpu
from jax.sharding import PartitionSpec as P

D = 8192
TOK_GRP = 768

momentum_decay = 0.9
step_size = 0.5
MESH = pl.DeviceIdType.MESH
f32, bf16 = jnp.float32, jnp.bfloat16


def kernel(
    n_group, n_mp, chunks, steps,
    pw_ref, rw_ref, mix_ref, x_hbm, tgt_hbm, num_hbm, mom_hbm, rec_hbm,
    fnum_hbm, frec_hbm, vr_hbm, fw_ref, frw_ref,
    x, xt, cur, vel, arr, tgt, part, sib, pair, peers, res, out, sc, val, wsend, wrecv,
    load_sem, sib_send, sib_recv, rs_send, rs_recv, ag_send, ag_recv, fwd_send, fwd_recv,
    msg_send, msg_recv, relay_send, w_send, w_recv, store_sem,
):
    row_scale = 1.0 / math.sqrt(D)
    grad_scale = 1.0 / math.sqrt(TOK_GRP)
    nz = n_mp // 2
    rows, width = x.shape[1], x.shape[2]
    own = rows // n_mp
    cols = cur.shape[2]
    jobs = steps * chunks
    g = lax.axis_index("group")
    m = lax.axis_index("mp")
    z = m // 2
    core = m % 2
    other = 1 - core
    odd = g % 2

    def relayed(c):
        return n_group % 2 == 0 and n_group > 2 and c % 2 == 1

    sibling = z * 2 + other

    def z_peer(d):
        return lax.rem(z + d, nz) * 2 + core

    def g_peer(d):
        return lax.rem(g + d + n_group, n_group)

    def span(c):
        return pl.ds(c * cols, cols)

    loads = {}

    def load(name, src, dst):
        copy = pltpu.make_async_copy(src, dst, load_sem.at[len(loads)])
        copy.start()
        loads[name] = copy

    load("num0", num_hbm.at[0, :, span(0)], cur.at[0])
    load("x0", x_hbm.at[0], x.at[0])
    for c in range(1, chunks):
        load(f"num{c}", num_hbm.at[0, :, span(c)], cur.at[c])
    for s in range(steps):
        load(f"tgt{s}", tgt_hbm.at[s], tgt.at[s])
    for c in range(chunks):
        load(f"mom{c}", mom_hbm.at[0, :, span(c)], vel.at[c])
        load(f"rec{c}", rec_hbm.at[0, :, span(c)], arr.at[c])
    for s in range(1, steps):
        load(f"x{s}", x_hbm.at[s], x.at[s])

    barrier = pltpu.get_barrier_semaphore()
    offsets = []
    for s in range(steps):
        for d in (2**s, -(2**s)):
            if d % n_group and d % n_group not in offsets:
                offsets.append(d % n_group)
    for d in offsets:
        pl.semaphore_signal(barrier, inc=1, device_id={"group": g_peer(d)}, device_id_type=MESH)
    for d in range(1, nz):
        pl.semaphore_signal(barrier, inc=1, device_id={"mp": z_peer(d)}, device_id_type=MESH)
    pl.semaphore_signal(barrier, inc=1, device_id={"mp": sibling}, device_id_type=MESH)
    pl.semaphore_wait(barrier, len(offsets) + nz)

    keep = [mix_ref[0, s].astype(f32) / 8.0 for s in range(steps)]
    weights = [pw_ref[0], keep[0] * pw_ref[0] + rw_ref[0]]
    w_copies = []
    for s in range(steps):
        outgoing_weight = jnp.full(wsend.shape[1:], (1.0 - keep[s]) * weights[s], f32)
        wsend[s] = outgoing_weight.astype(bf16).astype(f32)
        copy = pltpu.make_async_remote_copy(
            wsend.at[s], wrecv.at[s], w_send.at[s], w_recv.at[s],
            device_id={"group": g_peer(2**s)}, device_id_type=MESH,
        )
        copy.start()
        w_copies.append(copy)

    sends, stores = [], []
    sib_c, rs_c, ag_c, fwd_c, msg_c = {}, {}, {}, {}, {}

    def remote(src, dst, send, recv, where):
        copy = pltpu.make_async_remote_copy(src, dst, send, recv, device_id=where, device_id_type=MESH)
        copy.start()
        sends.append(copy)
        return copy

    def forward(j):
        s, c = divmod(j, chunks)
        if s == 0:
            loads[f"num{c}"].wait()
        if j == 0:
            loads["x0"].wait()
        sc[...] = (cur[c].astype(f32) / weights[s]).astype(bf16)
        half_z = nz // 2
        tile = half_z * 2 * own

        def body(i, _):
            lhs = x[s, pl.ds(pl.multiple_of(i * tile, tile), tile), :]
            product = jnp.dot(lhs, sc[...], preferred_element_type=f32) * row_scale
            part[j, pl.ds(i * half_z, half_z)] = product.astype(bf16).reshape(half_z, 2, own, cols)
            return 0

        lax.fori_loop(0, 2, body, 0)
        sib_c[j] = remote(part.at[j, :, other], sib.at[j], sib_send.at[j], sib_recv.at[j], {"mp": sibling})

    def pair_sum(j):
        sib_c[j].wait_recv()
        for k in range(nz):
            pair[j, k] = (part[j, k, core].astype(f32) + sib[j, k].astype(f32)).astype(bf16)
        for d in range(1, nz):
            rs_c[j, d] = remote(
                pair.at[j, lax.rem(z + d, nz)], peers.at[j, d - 1],
                rs_send.at[j, d - 1], rs_recv.at[j, d - 1], {"mp": z_peer(d)},
            )

    def value(j):
        s, c = divmod(j, chunks)
        total = pair[j, z].astype(f32)
        for d in range(1, nz):
            rs_c[j, d].wait_recv()
            total += peers[j, d - 1].astype(f32)
        values = total.astype(bf16)
        columns = slice(c * cols, (c + 1) * cols)
        val[s, :, columns] = values
        if c == 0:
            loads[f"tgt{s}"].wait()
        res[j, z, core] = (values.astype(f32) - tgt[s, :, columns].astype(f32)).astype(bf16)
        for d in range(1, nz):
            ag_c[j, d] = remote(
                res.at[j, z, core], res.at[j, z, core],
                ag_send.at[j, d - 1], ag_recv.at[j, d - 1], {"mp": z_peer(d)},
            )
        if c == chunks - 1:
            store = pltpu.make_async_copy(val.at[s], vr_hbm.at[s], store_sem.at[s])
            store.start()
            stores.append(store)

    def pass_on(j):
        for d in range(1, nz):
            source = lax.rem(z - d + nz, nz)
            pltpu.make_async_remote_copy(
                res.at[j, z, core], res.at[j, source, core],
                ag_send.at[j, d - 1], ag_recv.at[j, d - 1],
                device_id={"mp": z_peer(d)}, device_id_type=MESH,
            ).wait_recv()
        remote(res.at[j, :, core], res.at[j, :, core], fwd_send.at[j], fwd_recv.at[j], {"mp": sibling})

    def update(j):
        s, c = divmod(j, chunks)
        pltpu.make_async_remote_copy(
            res.at[j, :, core], res.at[j, :, other], fwd_send.at[j], fwd_recv.at[j],
            device_id={"mp": sibling}, device_id_type=MESH,
        ).wait_recv()
        if s == 0:
            loads[f"mom{c}"].wait()
            loads[f"rec{c}"].wait()
        else:
            landing(j - chunks).wait_recv()
        tile = min(256, width)

        def body(i, _):
            at = pl.ds(pl.multiple_of(i * tile, tile), tile)
            gradient = jnp.dot(
                xt[s, at, :], res[j].reshape(rows, cols), preferred_element_type=f32
            ) * grad_scale
            velocity = momentum_decay * vel[c, at, :] + gradient
            vel[c, at, :] = velocity
            half_step = cur[c, at, :].astype(f32) - step_size * velocity
            out[j, at, :] = ((1.0 - keep[s]) * half_step).astype(bf16)
            landed = arr[c, at, :] if s == 0 else arr[chunks + c, at, :]
            cur[c, at, :] = (keep[s] * half_step + landed.astype(f32)).astype(bf16)
            return 0

        lax.fori_loop(0, width // tile, body, 0)
        if s == 0 and relayed(c):
            msg_c[j] = remote(
                out.at[j], arr.at[chunks + c + odd * chunks], msg_send.at[j],
                msg_recv.at[j + odd * jobs], {"group": g_peer(1 + odd)},
            )
        else:
            msg_c[j] = remote(
                out.at[j], arr.at[chunks + c if s == 0 else 3 * chunks + c],
                msg_send.at[j], msg_recv.at[j], {"group": g_peer(2**s)},
            )
        if s == steps - 1:
            store = pltpu.make_async_copy(cur.at[c], fnum_hbm.at[0, :, span(c)], store_sem.at[steps + c])
            store.start()
            stores.append(store)

    def landing(j):
        s, c = divmod(j, chunks)
        return pltpu.make_async_remote_copy(
            out.at[j], arr.at[chunks + c if s == 0 else 3 * chunks + c],
            msg_send.at[j], msg_recv.at[j],
            device_id={"group": g_peer(2**s)}, device_id_type=MESH,
        )

    def relay_copy(c):
        return pltpu.make_async_remote_copy(
            arr.at[2 * chunks + c], arr.at[chunks + c], relay_send.at[c], msg_recv.at[c],
            device_id={"group": g_peer(-1)}, device_id_type=MESH,
        )

    def relay(c):
        @pl.when(odd == 1)
        def _():
            pltpu.make_async_remote_copy(
                out.at[c], arr.at[2 * chunks + c], msg_send.at[c], msg_recv.at[c + jobs],
                device_id={"group": g_peer(2)}, device_id_type=MESH,
            ).wait_recv()
            relay_copy(c).start()

    def transpose(s, i, pieces):
        if s > 0 and i == 0:
            loads[f"x{s}"].wait()
        tile = width // pieces
        xt[s, i * tile:(i + 1) * tile, :] = x[s, :, i * tile:(i + 1) * tile].T

    stages = ((update, 6), (pass_on, 5), (value, 3), (pair_sum, 1), (forward, 0))
    depth = stages[0][1]
    first, second = list(range(chunks)), list(range(chunks, jobs))
    order = first[:depth]
    first = first[depth:]
    while second:
        order.append(second.pop(0))
        if first:
            order.append(first.pop(0))
    place = {j: i for i, j in enumerate(order)}
    for tick in range(jobs + depth):
        for stage, delay in stages:
            if 0 <= tick - delay < jobs:
                stage(order[tick - delay])
        for c in range(chunks):
            if relayed(c) and tick == place[c] + depth + 3:
                relay(c)
        for s in range(steps):
            if 0 <= tick - s * chunks // 2 < 4:
                transpose(s, tick - s * chunks // 2, 4)

    for copy in w_copies:
        copy.wait()
    fw_ref[...] = keep[1] * weights[1] + wrecv[0]
    frw_ref[...] = wrecv[1]
    for c in range(chunks):
        landing((steps - 1) * chunks + c).wait_recv()
        store = pltpu.make_async_copy(
            arr.at[3 * chunks + c], frec_hbm.at[0, :, span(c)], store_sem.at[steps + chunks + c]
        )
        store.start()
        stores.append(store)
    for copy in sends:
        copy.wait_send()
    for c in range(chunks):
        if relayed(c):
            @pl.when(odd == 1)
            def _():
                relay_copy(c).wait_send()
    for store in stores:
        store.wait()


def finish(fnum, frec, vr, fw, frw, fnum_out, fw_out, frec_out, frw_out, vr_out, hold, vr_hold, load_sem, store_sem):
    moves = []
    pieces, tile = hold.shape[1], hold.shape[2]
    for i, (src, dst) in enumerate(((fnum, fnum_out), (frec, frec_out))):
        for p in range(pieces):
            at = pl.ds(p * tile, tile)
            moves.append((src.at[0, at], hold.at[i, p], dst.at[0, at]))
    moves.append((vr, vr_hold, vr_out))
    loads, stores = [], []
    for i, (src, via, dst) in enumerate(moves):
        loads.append(pltpu.make_async_copy(src, via, load_sem.at[i]))
        stores.append(pltpu.make_async_copy(via, dst, store_sem.at[i]))
        loads[-1].start()
    fw_out[0] = fw[0, 0]
    frw_out[0] = frw[0, 0]
    for load, store in zip(loads, stores):
        load.wait()
        store.start()
    for store in stores:
        store.wait()


def local(inputs, targets, numerator, momentum, received, push_weight, received_weight, mix_share):
    steps, rows, width = inputs.shape
    own, kv = targets.shape[1], targets.shape[2]
    n_group, n_mp = lax.axis_size("group"), lax.axis_size("mp")
    chunks = 8
    cols = kv // chunks
    jobs = steps * chunks
    nz = n_mp // 2
    pieces = 4
    any_space = pl.BlockSpec(memory_space=pl.ANY)
    smem = pl.BlockSpec(memory_space=pltpu.SMEM)
    vmem = pl.BlockSpec(memory_space=pltpu.VMEM)
    dma = pltpu.SemaphoreType.DMA
    fnum, frec, vr, fw, frw = pl.pallas_call(
        functools.partial(kernel, n_group, n_mp, chunks, steps),
        out_shape=(
            jax.ShapeDtypeStruct(numerator.shape, bf16),
            jax.ShapeDtypeStruct(numerator.shape, bf16),
            jax.ShapeDtypeStruct(targets.shape, bf16),
            jax.ShapeDtypeStruct((8, 128), f32),
            jax.ShapeDtypeStruct((8, 128), f32),
        ),
        in_specs=[smem] * 3 + [any_space] * 5,
        out_specs=(any_space, any_space, any_space, vmem, vmem),
        scratch_shapes=[
            pltpu.VMEM((steps, rows, width), bf16),
            pltpu.VMEM((steps, width, rows), bf16),
            pltpu.VMEM((chunks, width, cols), bf16),
            pltpu.VMEM((chunks, width, cols), f32),
            pltpu.VMEM((4 * chunks, width, cols), bf16),
            pltpu.VMEM((steps, own, kv), bf16),
            pltpu.VMEM((jobs, nz, 2, own, cols), bf16),
            pltpu.VMEM((jobs, nz, own, cols), bf16),
            pltpu.VMEM((jobs, nz, own, cols), bf16),
            pltpu.VMEM((jobs, nz - 1, own, cols), bf16),
            pltpu.VMEM((jobs, nz, 2, own, cols), bf16),
            pltpu.VMEM((jobs, width, cols), bf16),
            pltpu.VMEM((width, cols), bf16),
            pltpu.VMEM((steps, own, kv), bf16),
            pltpu.VMEM((steps, 8, 128), f32),
            pltpu.VMEM((steps, 8, 128), f32),
            dma((3 * chunks + 2 * steps,)),
            dma((jobs,)), dma((jobs,)),
            dma((jobs, nz - 1)), dma((jobs, nz - 1)),
            dma((jobs, nz - 1)), dma((jobs, nz - 1)),
            dma((jobs,)), dma((jobs,)),
            dma((jobs,)), dma((2 * jobs,)), dma((chunks,)),
            dma((steps,)), dma((steps,)),
            dma((steps + 2 * chunks,)),
        ],
        compiler_params=pltpu.CompilerParams(
            collective_id=0, has_side_effects=True, vmem_limit_bytes=58 * 1024 * 1024
        ),
    )(push_weight, received_weight, mix_share, inputs, targets, numerator, momentum, received)
    return pl.pallas_call(
        finish,
        out_shape=(
            jax.ShapeDtypeStruct(numerator.shape, bf16),
            jax.ShapeDtypeStruct(push_weight.shape, f32),
            jax.ShapeDtypeStruct(numerator.shape, bf16),
            jax.ShapeDtypeStruct(push_weight.shape, f32),
            jax.ShapeDtypeStruct(targets.shape, bf16),
        ),
        in_specs=[any_space, any_space, any_space, vmem, vmem],
        out_specs=(any_space, smem, any_space, smem, any_space),
        scratch_shapes=[
            pltpu.VMEM((2, pieces, width // pieces, kv), bf16),
            pltpu.VMEM(targets.shape, bf16),
            dma((2 * pieces + 1,)), dma((2 * pieces + 1,)),
        ],
        compiler_params=pltpu.CompilerParams(vmem_limit_bytes=16 * 1024 * 1024),
    )(fnum, frec, vr, fw, frw)


def solution(mesh):
    placed = (
        P(None, "group", "mp"),
        P(None, ("group", "mp"), None),
        P("group", "mp", None),
        P("group", "mp", None),
        P("group", "mp", None),
        P("group"),
        P("group"),
        P("group", None),
    )
    return jax.shard_map(
        local,
        mesh=mesh,
        in_specs=placed,
        out_specs=(
            P("group", "mp", None),
            P("group"),
            P("group", "mp", None),
            P("group"),
            P(None, ("group", "mp"), None),
        ),
        check_vma=False,
    )
```

```python
import functools
import math

import jax
import jax.numpy as jnp
from jax import lax
from jax.experimental import pallas as pl
from jax.experimental.pallas import tpu as pltpu
from jax.sharding import PartitionSpec as P

D = 8192
TOK_GRP = 768

momentum_decay = 0.9
step_size = 0.5
MESH = pl.DeviceIdType.MESH
f32, bf16 = jnp.float32, jnp.bfloat16
CHUNKS = 8
SCHEDULE = (
    (0, 0), (0, 1), (0, 2), (1, 0), (1, 1), (0, 3), (1, 2), (5, 0), (5, 1), (5, 2), (1, 3), (2, 0),
    (5, 3), (5, 4), (5, 5), (2, 1), (5, 6), (5, 7), (2, 2), (2, 3), (3, 0), (4, 0), (3, 1), (0, 8),
    (3, 2), (0, 4), (4, 1), (4, 2), (3, 3), (1, 8), (1, 4), (0, 9), (4, 3), (0, 5), (2, 8), (6, 1),
    (1, 9), (0, 10), (2, 4), (1, 5), (0, 6), (3, 8), (1, 10), (1, 6), (4, 8), (6, 3), (3, 4), (2, 9),
    (0, 11), (4, 4), (2, 5), (2, 10), (1, 11), (0, 7), (2, 6), (3, 9), (1, 7), (4, 9), (3, 5), (0, 12),
    (3, 10), (4, 5), (4, 10), (3, 6), (2, 11), (1, 12), (0, 13), (4, 6), (2, 7), (1, 13), (3, 11), (0, 14),
    (6, 5), (2, 12), (4, 11), (3, 7), (1, 14), (2, 13), (4, 7), (3, 12), (0, 15), (4, 12), (2, 14), (3, 13),
    (1, 15), (4, 13), (6, 7), (3, 14), (4, 14), (2, 15), (3, 15), (4, 15),
)


def kernel(
    n_group, n_mp, chunks, steps,
    pw_ref, rw_ref, mix_ref, x_hbm, tgt_hbm, num_hbm, mom_hbm, rec_hbm,
    fnum_hbm, frec_hbm, vr_hbm, fw_ref, frw_ref,
    x, xt, cur, vel, arr, tgt, part, sib, pair, peers, res, out, sc, val, wsend, wrecv,
    load_sem, sib_send, sib_recv, rs_send, rs_recv, ag_send, ag_recv, fwd_send, fwd_recv,
    msg_send, msg_recv, relay_send, w_send, w_recv, store_sem,
):
    row_scale = 1.0 / math.sqrt(D)
    grad_scale = 1.0 / math.sqrt(TOK_GRP)
    nz = n_mp // 2
    rows, width = x.shape[1], x.shape[2]
    own = rows // n_mp
    cols = cur.shape[2]
    jobs = steps * chunks
    g = lax.axis_index("group")
    m = lax.axis_index("mp")
    z = m // 2
    core = m % 2
    other = 1 - core
    odd = g % 2

    def relayed(c):
        return n_group % 2 == 0 and n_group > 2 and c % 2 == 1

    sibling = z * 2 + other

    def z_peer(d):
        return lax.rem(z + d, nz) * 2 + core

    def g_peer(d):
        return lax.rem(g + d + n_group, n_group)

    def span(c):
        return pl.ds(c * cols, cols)

    loads = {}

    def load(name, src, dst):
        copy = pltpu.make_async_copy(src, dst, load_sem.at[len(loads)])
        copy.start()
        loads[name] = copy

    load("num0", num_hbm.at[0, :, span(0)], cur.at[0])
    load("x0", x_hbm.at[0], x.at[0])
    for c in range(1, chunks):
        load(f"num{c}", num_hbm.at[0, :, span(c)], cur.at[c])
    for s in range(steps):
        load(f"tgt{s}", tgt_hbm.at[s], tgt.at[s])
    for c in range(chunks):
        load(f"mom{c}", mom_hbm.at[0, :, span(c)], vel.at[c])
        load(f"rec{c}", rec_hbm.at[0, :, span(c)], arr.at[c])
    for s in range(1, steps):
        load(f"x{s}", x_hbm.at[s], x.at[s])

    barrier = pltpu.get_barrier_semaphore()
    offsets = []
    for s in range(steps):
        for d in (2**s, -(2**s)):
            if d % n_group and d % n_group not in offsets:
                offsets.append(d % n_group)
    for d in offsets:
        pl.semaphore_signal(barrier, inc=1, device_id={"group": g_peer(d)}, device_id_type=MESH)
    for d in range(1, nz):
        pl.semaphore_signal(barrier, inc=1, device_id={"mp": z_peer(d)}, device_id_type=MESH)
    pl.semaphore_signal(barrier, inc=1, device_id={"mp": sibling}, device_id_type=MESH)
    pl.semaphore_wait(barrier, len(offsets) + nz)

    keep = [mix_ref[0, s].astype(f32) / 8.0 for s in range(steps)]
    weights = [pw_ref[0], keep[0] * pw_ref[0] + rw_ref[0]]
    w_copies = []
    for s in range(steps):
        outgoing_weight = jnp.full(wsend.shape[1:], (1.0 - keep[s]) * weights[s], f32)
        wsend[s] = outgoing_weight.astype(bf16).astype(f32)
        copy = pltpu.make_async_remote_copy(
            wsend.at[s], wrecv.at[s], w_send.at[s], w_recv.at[s],
            device_id={"group": g_peer(2**s)}, device_id_type=MESH,
        )
        copy.start()
        w_copies.append(copy)

    sends, stores = [], []
    sib_c, rs_c, ag_c, fwd_c, msg_c = {}, {}, {}, {}, {}

    def remote(src, dst, send, recv, where):
        copy = pltpu.make_async_remote_copy(src, dst, send, recv, device_id=where, device_id_type=MESH)
        copy.start()
        sends.append(copy)
        return copy

    def forward(j):
        s, c = divmod(j, chunks)
        if s == 0:
            loads[f"num{c}"].wait()
        if j == 0:
            loads["x0"].wait()
        sc[...] = (cur[c].astype(f32) / weights[s]).astype(bf16)
        half_z = nz // 2
        tile = half_z * 2 * own

        def body(i, _):
            lhs = x[s, pl.ds(pl.multiple_of(i * tile, tile), tile), :]
            product = jnp.dot(lhs, sc[...], preferred_element_type=f32) * row_scale
            part[j, pl.ds(i * half_z, half_z)] = product.astype(bf16).reshape(half_z, 2, own, cols)
            return 0

        lax.fori_loop(0, 2, body, 0)
        sib_c[j] = remote(part.at[j, :, other], sib.at[j], sib_send.at[j], sib_recv.at[j], {"mp": sibling})

    def pair_sum(j):
        sib_c[j].wait_recv()
        for k in range(nz):
            pair[j, k] = (part[j, k, core].astype(f32) + sib[j, k].astype(f32)).astype(bf16)
        for d in range(1, nz):
            rs_c[j, d] = remote(
                pair.at[j, lax.rem(z + d, nz)], peers.at[j, d - 1],
                rs_send.at[j, d - 1], rs_recv.at[j, d - 1], {"mp": z_peer(d)},
            )

    def value(j):
        s, c = divmod(j, chunks)
        total = pair[j, z].astype(f32)
        for d in range(1, nz):
            rs_c[j, d].wait_recv()
            total += peers[j, d - 1].astype(f32)
        values = total.astype(bf16)
        columns = slice(c * cols, (c + 1) * cols)
        val[s, :, columns] = values
        if c == 0:
            loads[f"tgt{s}"].wait()
        res[j, z, core] = (values.astype(f32) - tgt[s, :, columns].astype(f32)).astype(bf16)
        for d in range(1, nz):
            ag_c[j, d] = remote(
                res.at[j, z, core], res.at[j, z, core],
                ag_send.at[j, d - 1], ag_recv.at[j, d - 1], {"mp": z_peer(d)},
            )
        if c == chunks - 1:
            store = pltpu.make_async_copy(val.at[s], vr_hbm.at[s], store_sem.at[s])
            store.start()
            stores.append(store)

    def pass_on(j):
        for d in range(1, nz):
            source = lax.rem(z - d + nz, nz)
            pltpu.make_async_remote_copy(
                res.at[j, z, core], res.at[j, source, core],
                ag_send.at[j, d - 1], ag_recv.at[j, d - 1],
                device_id={"mp": z_peer(d)}, device_id_type=MESH,
            ).wait_recv()
        remote(res.at[j, :, core], res.at[j, :, core], fwd_send.at[j], fwd_recv.at[j], {"mp": sibling})

    def update(j):
        s, c = divmod(j, chunks)
        pltpu.make_async_remote_copy(
            res.at[j, :, core], res.at[j, :, other], fwd_send.at[j], fwd_recv.at[j],
            device_id={"mp": sibling}, device_id_type=MESH,
        ).wait_recv()
        if s == 0:
            loads[f"mom{c}"].wait()
            loads[f"rec{c}"].wait()
        else:
            landing(j - chunks).wait_recv()
        tile = min(256, width)

        def body(i, _):
            at = pl.ds(pl.multiple_of(i * tile, tile), tile)
            gradient = jnp.dot(
                xt[s, at, :], res[j].reshape(rows, cols), preferred_element_type=f32
            ) * grad_scale
            velocity = momentum_decay * vel[c, at, :] + gradient
            vel[c, at, :] = velocity
            half_step = cur[c, at, :].astype(f32) - step_size * velocity
            out[j, at, :] = ((1.0 - keep[s]) * half_step).astype(bf16)
            landed = arr[c, at, :] if s == 0 else arr[chunks + c, at, :]
            cur[c, at, :] = (keep[s] * half_step + landed.astype(f32)).astype(bf16)
            return 0

        lax.fori_loop(0, width // tile, body, 0)
        if s == 0 and relayed(c):
            msg_c[j] = remote(
                out.at[j], arr.at[chunks + c + odd * chunks], msg_send.at[j],
                msg_recv.at[j + odd * jobs], {"group": g_peer(1 + odd)},
            )
        else:
            msg_c[j] = remote(
                out.at[j], arr.at[chunks + c if s == 0 else 3 * chunks + c],
                msg_send.at[j], msg_recv.at[j], {"group": g_peer(2**s)},
            )
        if s == steps - 1:
            store = pltpu.make_async_copy(cur.at[c], fnum_hbm.at[0, :, span(c)], store_sem.at[steps + c])
            store.start()
            stores.append(store)

    def landing(j):
        s, c = divmod(j, chunks)
        return pltpu.make_async_remote_copy(
            out.at[j], arr.at[chunks + c if s == 0 else 3 * chunks + c],
            msg_send.at[j], msg_recv.at[j],
            device_id={"group": g_peer(2**s)}, device_id_type=MESH,
        )

    def relay_copy(c):
        return pltpu.make_async_remote_copy(
            arr.at[2 * chunks + c], arr.at[chunks + c], relay_send.at[c], msg_recv.at[c],
            device_id={"group": g_peer(-1)}, device_id_type=MESH,
        )

    def relay(c):
        if not relayed(c):
            return

        @pl.when(odd == 1)
        def _():
            pltpu.make_async_remote_copy(
                out.at[c], arr.at[2 * chunks + c], msg_send.at[c], msg_recv.at[c + jobs],
                device_id={"group": g_peer(2)}, device_id_type=MESH,
            ).wait_recv()
            relay_copy(c).start()

    def transpose(index):
        s, i = divmod(index, 4)
        if s > 0 and i == 0:
            loads[f"x{s}"].wait()
        tile = width // 4
        xt[s, i * tile:(i + 1) * tile, :] = x[s, :, i * tile:(i + 1) * tile].T

    stages = (forward, pair_sum, value, pass_on, update, transpose, relay)
    for stage, index in SCHEDULE:
        stages[stage](index)

    for copy in w_copies:
        copy.wait()
    fw_ref[...] = keep[1] * weights[1] + wrecv[0]
    frw_ref[...] = wrecv[1]
    for c in range(chunks):
        landing((steps - 1) * chunks + c).wait_recv()
        store = pltpu.make_async_copy(
            arr.at[3 * chunks + c], frec_hbm.at[0, :, span(c)], store_sem.at[steps + chunks + c]
        )
        store.start()
        stores.append(store)
    for copy in sends:
        copy.wait_send()
    for c in range(chunks):
        if relayed(c):
            @pl.when(odd == 1)
            def _():
                relay_copy(c).wait_send()
    for store in stores:
        store.wait()


def finish(fnum, frec, vr, fw, frw, fnum_out, fw_out, frec_out, frw_out, vr_out, hold, vr_hold, load_sem, store_sem):
    moves = []
    pieces, tile = hold.shape[1], hold.shape[2]
    for i, (src, dst) in enumerate(((fnum, fnum_out), (frec, frec_out))):
        for p in range(pieces):
            at = pl.ds(p * tile, tile)
            moves.append((src.at[0, at], hold.at[i, p], dst.at[0, at]))
    moves.append((vr, vr_hold, vr_out))
    loads, stores = [], []
    for i, (src, via, dst) in enumerate(moves):
        loads.append(pltpu.make_async_copy(src, via, load_sem.at[i]))
        stores.append(pltpu.make_async_copy(via, dst, store_sem.at[i]))
        loads[-1].start()
    fw_out[0] = fw[0, 0]
    frw_out[0] = frw[0, 0]
    for load, store in zip(loads, stores):
        load.wait()
        store.start()
    for store in stores:
        store.wait()


def local(inputs, targets, numerator, momentum, received, push_weight, received_weight, mix_share):
    steps, rows, width = inputs.shape
    own, kv = targets.shape[1], targets.shape[2]
    n_group, n_mp = lax.axis_size("group"), lax.axis_size("mp")
    chunks = CHUNKS
    cols = kv // chunks
    jobs = steps * chunks
    nz = n_mp // 2
    pieces = 4
    any_space = pl.BlockSpec(memory_space=pl.ANY)
    smem = pl.BlockSpec(memory_space=pltpu.SMEM)
    vmem = pl.BlockSpec(memory_space=pltpu.VMEM)
    dma = pltpu.SemaphoreType.DMA
    fnum, frec, vr, fw, frw = pl.pallas_call(
        functools.partial(kernel, n_group, n_mp, chunks, steps),
        out_shape=(
            jax.ShapeDtypeStruct(numerator.shape, bf16),
            jax.ShapeDtypeStruct(numerator.shape, bf16),
            jax.ShapeDtypeStruct(targets.shape, bf16),
            jax.ShapeDtypeStruct((8, 128), f32),
            jax.ShapeDtypeStruct((8, 128), f32),
        ),
        in_specs=[smem] * 3 + [any_space] * 5,
        out_specs=(any_space, any_space, any_space, vmem, vmem),
        scratch_shapes=[
            pltpu.VMEM((steps, rows, width), bf16),
            pltpu.VMEM((steps, width, rows), bf16),
            pltpu.VMEM((chunks, width, cols), bf16),
            pltpu.VMEM((chunks, width, cols), f32),
            pltpu.VMEM((4 * chunks, width, cols), bf16),
            pltpu.VMEM((steps, own, kv), bf16),
            pltpu.VMEM((jobs, nz, 2, own, cols), bf16),
            pltpu.VMEM((jobs, nz, own, cols), bf16),
            pltpu.VMEM((jobs, nz, own, cols), bf16),
            pltpu.VMEM((jobs, nz - 1, own, cols), bf16),
            pltpu.VMEM((jobs, nz, 2, own, cols), bf16),
            pltpu.VMEM((jobs, width, cols), bf16),
            pltpu.VMEM((width, cols), bf16),
            pltpu.VMEM((steps, own, kv), bf16),
            pltpu.VMEM((steps, 8, 128), f32),
            pltpu.VMEM((steps, 8, 128), f32),
            dma((3 * chunks + 2 * steps,)),
            dma((jobs,)), dma((jobs,)),
            dma((jobs, nz - 1)), dma((jobs, nz - 1)),
            dma((jobs, nz - 1)), dma((jobs, nz - 1)),
            dma((jobs,)), dma((jobs,)),
            dma((jobs,)), dma((2 * jobs,)), dma((chunks,)),
            dma((steps,)), dma((steps,)),
            dma((steps + 2 * chunks,)),
        ],
        compiler_params=pltpu.CompilerParams(
            collective_id=0, has_side_effects=True, vmem_limit_bytes=58 * 1024 * 1024
        ),
    )(push_weight, received_weight, mix_share, inputs, targets, numerator, momentum, received)
    return pl.pallas_call(
        finish,
        out_shape=(
            jax.ShapeDtypeStruct(numerator.shape, bf16),
            jax.ShapeDtypeStruct(push_weight.shape, f32),
            jax.ShapeDtypeStruct(numerator.shape, bf16),
            jax.ShapeDtypeStruct(push_weight.shape, f32),
            jax.ShapeDtypeStruct(targets.shape, bf16),
        ),
        in_specs=[any_space, any_space, any_space, vmem, vmem],
        out_specs=(any_space, smem, any_space, smem, any_space),
        scratch_shapes=[
            pltpu.VMEM((2, pieces, width // pieces, kv), bf16),
            pltpu.VMEM(targets.shape, bf16),
            dma((2 * pieces + 1,)), dma((2 * pieces + 1,)),
        ],
        compiler_params=pltpu.CompilerParams(vmem_limit_bytes=58 * 1024 * 1024),
    )(fnum, frec, vr, fw, frw)


def solution(mesh):
    placed = (
        P(None, "group", "mp"),
        P(None, ("group", "mp"), None),
        P("group", "mp", None),
        P("group", "mp", None),
        P("group", "mp", None),
        P("group"),
        P("group"),
        P("group", None),
    )
    return jax.shard_map(
        local,
        mesh=mesh,
        in_specs=placed,
        out_specs=(
            P("group", "mp", None),
            P("group"),
            P("group", "mp", None),
            P("group"),
            P(None, ("group", "mp"), None),
        ),
        check_vma=False,
    )
```

```python
import functools
import math

import jax
import jax.numpy as jnp
from jax import lax
from jax.experimental import pallas as pl
from jax.experimental.pallas import tpu as pltpu
from jax.sharding import PartitionSpec as P

D = 8192
TOK_GRP = 768

momentum_decay = 0.9
step_size = 0.5
MESH = pl.DeviceIdType.MESH
f32, bf16 = jnp.float32, jnp.bfloat16


def kernel(
    n_group, n_mp, chunks, steps,
    pw_ref, rw_ref, mix_ref, x_hbm, tgt_hbm, num_hbm, mom_hbm, rec_hbm,
    fnum_hbm, frec_hbm, vr_hbm, fw_ref, frw_ref,
    x, xt, cur, vel, arr, tgt, part, sib, pair, peers, res, out, sc, val, wsend, wrecv,
    load_sem, sib_send, sib_recv, rs_send, rs_recv, ag_send, ag_recv, fwd_send, fwd_recv,
    msg_send, msg_recv, relay_send, w_send, w_recv, store_sem,
):
    row_scale = 1.0 / math.sqrt(D)
    grad_scale = 1.0 / math.sqrt(TOK_GRP)
    nz = n_mp // 2
    rows, width = x.shape[1], x.shape[2]
    own = rows // n_mp
    cols = cur.shape[2]
    jobs = steps * chunks
    g = lax.axis_index("group")
    m = lax.axis_index("mp")
    z = m // 2
    core = m % 2
    other = 1 - core
    odd = g % 2

    def relayed(c):
        return n_group % 2 == 0 and n_group > 2 and c % 2 == 1

    sibling = z * 2 + other

    def z_peer(d):
        return lax.rem(z + d, nz) * 2 + core

    def g_peer(d):
        return lax.rem(g + d + n_group, n_group)

    def span(c):
        return pl.ds(c * cols, cols)

    loads = {}

    def load(name, src, dst):
        copy = pltpu.make_async_copy(src, dst, load_sem.at[len(loads)])
        copy.start()
        loads[name] = copy

    load("num0", num_hbm.at[0, :, span(0)], cur.at[0])
    load("x0", x_hbm.at[0], x.at[0])
    for c in range(1, chunks):
        load(f"num{c}", num_hbm.at[0, :, span(c)], cur.at[c])
    for s in range(steps):
        load(f"tgt{s}", tgt_hbm.at[s], tgt.at[s])
    for c in range(chunks):
        load(f"mom{c}", mom_hbm.at[0, :, span(c)], vel.at[c])
        load(f"rec{c}", rec_hbm.at[0, :, span(c)], arr.at[c])
    for s in range(1, steps):
        load(f"x{s}", x_hbm.at[s], x.at[s])

    barrier = pltpu.get_barrier_semaphore()
    offsets = []
    for s in range(steps):
        for d in (2**s, -(2**s)):
            if d % n_group and d % n_group not in offsets:
                offsets.append(d % n_group)
    for d in offsets:
        pl.semaphore_signal(barrier, inc=1, device_id={"group": g_peer(d)}, device_id_type=MESH)
    for d in range(1, nz):
        pl.semaphore_signal(barrier, inc=1, device_id={"mp": z_peer(d)}, device_id_type=MESH)
    pl.semaphore_signal(barrier, inc=1, device_id={"mp": sibling}, device_id_type=MESH)
    pl.semaphore_wait(barrier, len(offsets) + nz)

    keep = [mix_ref[0, s].astype(f32) / 8.0 for s in range(steps)]
    weights = [pw_ref[0], keep[0] * pw_ref[0] + rw_ref[0]]
    w_copies = []
    for s in range(steps):
        outgoing_weight = jnp.full(wsend.shape[1:], (1.0 - keep[s]) * weights[s], f32)
        wsend[s] = outgoing_weight.astype(bf16).astype(f32)
        copy = pltpu.make_async_remote_copy(
            wsend.at[s], wrecv.at[s], w_send.at[s], w_recv.at[s],
            device_id={"group": g_peer(2**s)}, device_id_type=MESH,
        )
        copy.start()
        w_copies.append(copy)

    sends, stores = [], []
    sib_c, rs_c, ag_c, fwd_c, msg_c = {}, {}, {}, {}, {}

    def remote(src, dst, send, recv, where):
        copy = pltpu.make_async_remote_copy(src, dst, send, recv, device_id=where, device_id_type=MESH)
        copy.start()
        sends.append(copy)
        return copy

    def forward(j):
        s, c = divmod(j, chunks)
        if s == 0:
            loads[f"num{c}"].wait()
        if j == 0:
            loads["x0"].wait()
        sc[...] = (cur[c].astype(f32) / weights[s]).astype(bf16)
        half_z = nz // 2
        tile = half_z * 2 * own

        def body(i, _):
            lhs = x[s, pl.ds(pl.multiple_of(i * tile, tile), tile), :]
            product = jnp.dot(lhs, sc[...], preferred_element_type=f32) * row_scale
            part[j, pl.ds(i * half_z, half_z)] = product.astype(bf16).reshape(half_z, 2, own, cols)
            return 0

        lax.fori_loop(0, 2, body, 0, unroll=True)
        sib_c[j] = remote(part.at[j, :, other], sib.at[j], sib_send.at[j], sib_recv.at[j], {"mp": sibling})

    def pair_sum(j):
        sib_c[j].wait_recv()
        for k in range(nz):
            pair[j, k] = (part[j, k, core].astype(f32) + sib[j, k].astype(f32)).astype(bf16)
        for d in range(1, nz):
            rs_c[j, d] = remote(
                pair.at[j, lax.rem(z + d, nz)], peers.at[j, d - 1],
                rs_send.at[j, d - 1], rs_recv.at[j, d - 1], {"mp": z_peer(d)},
            )

    def value(j):
        s, c = divmod(j, chunks)
        total = pair[j, z].astype(f32)
        for d in range(1, nz):
            rs_c[j, d].wait_recv()
            total += peers[j, d - 1].astype(f32)
        values = total.astype(bf16)
        columns = slice(c * cols, (c + 1) * cols)
        val[s, :, columns] = values
        if c == 0:
            loads[f"tgt{s}"].wait()
        res[j, z, core] = (values.astype(f32) - tgt[s, :, columns].astype(f32)).astype(bf16)
        for d in range(1, nz):
            ag_c[j, d] = remote(
                res.at[j, z, core], res.at[j, z, core],
                ag_send.at[j, d - 1], ag_recv.at[j, d - 1], {"mp": z_peer(d)},
            )
        if c == chunks - 1:
            store = pltpu.make_async_copy(val.at[s], vr_hbm.at[s], store_sem.at[s])
            store.start()
            stores.append(store)

    def pass_on(j):
        for d in range(1, nz):
            source = lax.rem(z - d + nz, nz)
            pltpu.make_async_remote_copy(
                res.at[j, z, core], res.at[j, source, core],
                ag_send.at[j, d - 1], ag_recv.at[j, d - 1],
                device_id={"mp": z_peer(d)}, device_id_type=MESH,
            ).wait_recv()
        remote(res.at[j, :, core], res.at[j, :, core], fwd_send.at[j], fwd_recv.at[j], {"mp": sibling})

    def update(j):
        s, c = divmod(j, chunks)
        pltpu.make_async_remote_copy(
            res.at[j, :, core], res.at[j, :, other], fwd_send.at[j], fwd_recv.at[j],
            device_id={"mp": sibling}, device_id_type=MESH,
        ).wait_recv()
        if s == 0:
            loads[f"mom{c}"].wait()
            loads[f"rec{c}"].wait()
        else:
            landing(j - chunks).wait_recv()
        tile = min(256, width)

        def body(i, _):
            at = pl.ds(pl.multiple_of(i * tile, tile), tile)
            gradient = jnp.dot(
                xt[s, at, :], res[j].reshape(rows, cols), preferred_element_type=f32
            ) * grad_scale
            velocity = momentum_decay * vel[c, at, :] + gradient
            if s < steps - 1:
                vel[c, at, :] = velocity
            half_step = cur[c, at, :].astype(f32) - step_size * velocity
            out[j, at, :] = ((1.0 - keep[s]) * half_step).astype(bf16)
            landed = arr[c, at, :] if s == 0 else arr[chunks + c, at, :]
            cur[c, at, :] = (keep[s] * half_step + landed.astype(f32)).astype(bf16)
            return 0

        lax.fori_loop(0, width // tile, body, 0, unroll=True)
        if s == 0 and relayed(c):
            msg_c[j] = remote(
                out.at[j], arr.at[chunks + c + odd * chunks], msg_send.at[j],
                msg_recv.at[j + odd * jobs], {"group": g_peer(1 + odd)},
            )
        else:
            msg_c[j] = remote(
                out.at[j], arr.at[chunks + c if s == 0 else 3 * chunks + c],
                msg_send.at[j], msg_recv.at[j], {"group": g_peer(2**s)},
            )
        if s == steps - 1:
            store = pltpu.make_async_copy(cur.at[c], fnum_hbm.at[0, :, span(c)], store_sem.at[steps + c])
            store.start()
            stores.append(store)

    def landing(j):
        s, c = divmod(j, chunks)
        return pltpu.make_async_remote_copy(
            out.at[j], arr.at[chunks + c if s == 0 else 3 * chunks + c],
            msg_send.at[j], msg_recv.at[j],
            device_id={"group": g_peer(2**s)}, device_id_type=MESH,
        )

    def relay_copy(c):
        return pltpu.make_async_remote_copy(
            arr.at[2 * chunks + c], arr.at[chunks + c], relay_send.at[c], msg_recv.at[c],
            device_id={"group": g_peer(-1)}, device_id_type=MESH,
        )

    def relay(c):
        @pl.when(odd == 1)
        def _():
            pltpu.make_async_remote_copy(
                out.at[c], arr.at[2 * chunks + c], msg_send.at[c], msg_recv.at[c + jobs],
                device_id={"group": g_peer(2)}, device_id_type=MESH,
            ).wait_recv()
            relay_copy(c).start()

    def transpose(s, i, pieces):
        if s > 0 and i == 0:
            loads[f"x{s}"].wait()
        tile = width // pieces
        xt[s, i * tile:(i + 1) * tile, :] = x[s, :, i * tile:(i + 1) * tile].T

    stages = ((update, 6), (pass_on, 5), (value, 3), (pair_sum, 1), (forward, 0))
    depth = stages[0][1]
    first, second = list(range(chunks)), list(range(chunks, jobs))
    order = first[:depth]
    first = first[depth:]
    while second:
        order.append(second.pop(0))
        if first:
            order.append(first.pop(0))
    place = {j: i for i, j in enumerate(order)}
    for tick in range(jobs + depth):
        for stage, delay in stages:
            if 0 <= tick - delay < jobs:
                stage(order[tick - delay])
        for c in range(chunks):
            if relayed(c) and tick == place[c] + depth + 3:
                relay(c)
        for s in range(steps):
            if 0 <= tick - s * chunks // 2 < 4:
                transpose(s, tick - s * chunks // 2, 4)

    for copy in w_copies:
        copy.wait()
    fw_ref[...] = keep[1] * weights[1] + wrecv[0]
    frw_ref[...] = wrecv[1]
    for c in range(chunks):
        landing((steps - 1) * chunks + c).wait_recv()
        store = pltpu.make_async_copy(
            arr.at[3 * chunks + c], frec_hbm.at[0, :, span(c)], store_sem.at[steps + chunks + c]
        )
        store.start()
        stores.append(store)
    for copy in sends:
        copy.wait_send()
    for c in range(chunks):
        if relayed(c):
            @pl.when(odd == 1)
            def _():
                relay_copy(c).wait_send()
    for store in stores:
        store.wait()


def finish(fnum, frec, vr, fw, frw, fnum_out, fw_out, frec_out, frw_out, vr_out, hold, vr_hold, load_sem, store_sem):
    moves = []
    pieces, tile = hold.shape[1], hold.shape[2]
    for i, (src, dst) in enumerate(((fnum, fnum_out), (frec, frec_out))):
        for p in range(pieces):
            at = pl.ds(p * tile, tile)
            moves.append((src.at[0, at], hold.at[i, p], dst.at[0, at]))
    moves.append((vr, vr_hold, vr_out))
    loads, stores = [], []
    for i, (src, via, dst) in enumerate(moves):
        loads.append(pltpu.make_async_copy(src, via, load_sem.at[i]))
        stores.append(pltpu.make_async_copy(via, dst, store_sem.at[i]))
        loads[-1].start()
    fw_out[0] = fw[0, 0]
    frw_out[0] = frw[0, 0]
    for load, store in zip(loads, stores):
        load.wait()
        store.start()
    for store in stores:
        store.wait()


def local(inputs, targets, numerator, momentum, received, push_weight, received_weight, mix_share):
    steps, rows, width = inputs.shape
    own, kv = targets.shape[1], targets.shape[2]
    n_group, n_mp = lax.axis_size("group"), lax.axis_size("mp")
    chunks = 8
    cols = kv // chunks
    jobs = steps * chunks
    nz = n_mp // 2
    pieces = 8
    any_space = pl.BlockSpec(memory_space=pl.ANY)
    smem = pl.BlockSpec(memory_space=pltpu.SMEM)
    vmem = pl.BlockSpec(memory_space=pltpu.VMEM)
    dma = pltpu.SemaphoreType.DMA
    fnum, frec, vr, fw, frw = pl.pallas_call(
        functools.partial(kernel, n_group, n_mp, chunks, steps),
        out_shape=(
            jax.ShapeDtypeStruct(numerator.shape, bf16),
            jax.ShapeDtypeStruct(numerator.shape, bf16),
            jax.ShapeDtypeStruct(targets.shape, bf16),
            jax.ShapeDtypeStruct((8, 128), f32),
            jax.ShapeDtypeStruct((8, 128), f32),
        ),
        in_specs=[smem] * 3 + [any_space] * 5,
        out_specs=(any_space, any_space, any_space, vmem, vmem),
        scratch_shapes=[
            pltpu.VMEM((steps, rows, width), bf16),
            pltpu.VMEM((steps, width, rows), bf16),
            pltpu.VMEM((chunks, width, cols), bf16),
            pltpu.VMEM((chunks, width, cols), f32),
            pltpu.VMEM((4 * chunks, width, cols), bf16),
            pltpu.VMEM((steps, own, kv), bf16),
            pltpu.VMEM((jobs, nz, 2, own, cols), bf16),
            pltpu.VMEM((jobs, nz, own, cols), bf16),
            pltpu.VMEM((jobs, nz, own, cols), bf16),
            pltpu.VMEM((jobs, nz - 1, own, cols), bf16),
            pltpu.VMEM((jobs, nz, 2, own, cols), bf16),
            pltpu.VMEM((jobs, width, cols), bf16),
            pltpu.VMEM((width, cols), bf16),
            pltpu.VMEM((steps, own, kv), bf16),
            pltpu.VMEM((steps, 8, 128), f32),
            pltpu.VMEM((steps, 8, 128), f32),
            dma((3 * chunks + 2 * steps,)),
            dma((jobs,)), dma((jobs,)),
            dma((jobs, nz - 1)), dma((jobs, nz - 1)),
            dma((jobs, nz - 1)), dma((jobs, nz - 1)),
            dma((jobs,)), dma((jobs,)),
            dma((jobs,)), dma((2 * jobs,)), dma((chunks,)),
            dma((steps,)), dma((steps,)),
            dma((steps + 2 * chunks,)),
        ],
        compiler_params=pltpu.CompilerParams(
            collective_id=0, has_side_effects=True, vmem_limit_bytes=58 * 1024 * 1024
        ),
    )(push_weight, received_weight, mix_share, inputs, targets, numerator, momentum, received)
    return pl.pallas_call(
        finish,
        out_shape=(
            jax.ShapeDtypeStruct(numerator.shape, bf16),
            jax.ShapeDtypeStruct(push_weight.shape, f32),
            jax.ShapeDtypeStruct(numerator.shape, bf16),
            jax.ShapeDtypeStruct(push_weight.shape, f32),
            jax.ShapeDtypeStruct(targets.shape, bf16),
        ),
        in_specs=[any_space, any_space, any_space, vmem, vmem],
        out_specs=(any_space, smem, any_space, smem, any_space),
        scratch_shapes=[
            pltpu.VMEM((2, pieces, width // pieces, kv), bf16),
            pltpu.VMEM(targets.shape, bf16),
            dma((2 * pieces + 1,)), dma((2 * pieces + 1,)),
        ],
        compiler_params=pltpu.CompilerParams(vmem_limit_bytes=58 * 1024 * 1024),
    )(fnum, frec, vr, fw, frw)


def solution(mesh):
    placed = (
        P(None, "group", "mp"),
        P(None, ("group", "mp"), None),
        P("group", "mp", None),
        P("group", "mp", None),
        P("group", "mp", None),
        P("group"),
        P("group"),
        P("group", None),
    )
    return jax.shard_map(
        local,
        mesh=mesh,
        in_specs=placed,
        out_specs=(
            P("group", "mp", None),
            P("group"),
            P("group", "mp", None),
            P("group"),
            P(None, ("group", "mp"), None),
        ),
        check_vma=False,
    )
```

```python
import functools
import math

import jax
import jax.numpy as jnp
from jax import lax
from jax.experimental import pallas as pl
from jax.experimental.pallas import tpu as pltpu
from jax.sharding import PartitionSpec as P

D = 8192
TOK_GRP = 768

momentum_decay = 0.9
step_size = 0.5
MESH = pl.DeviceIdType.MESH
f32, bf16 = jnp.float32, jnp.bfloat16


def kernel(
    n_group, n_mp, chunks, steps,
    pw_ref, rw_ref, mix_ref, x_hbm, tgt_hbm, num_hbm, mom_hbm, rec_hbm,
    fnum_hbm, frec_hbm, vr_hbm, fw_ref, frw_ref,
    x, xt, cur, vel, arr, tgt, part, sib, pair, peers, res, out, sc, val, wsend, wrecv,
    load_sem, sib_send, sib_recv, rs_send, rs_recv, ag_send, ag_recv, fwd_send, fwd_recv,
    msg_send, msg_recv, relay_send, w_send, w_recv, store_sem,
):
    row_scale = 1.0 / math.sqrt(D)
    grad_scale = 1.0 / math.sqrt(TOK_GRP)
    nz = n_mp // 2
    rows, width = x.shape[1], x.shape[2]
    own = rows // n_mp
    cols = cur.shape[2]
    jobs = steps * chunks
    g = lax.axis_index("group")
    m = lax.axis_index("mp")
    z = m // 2
    core = m % 2
    other = 1 - core
    odd = g % 2

    def relayed(c):
        return n_group % 2 == 0 and n_group > 2 and c % 2 == 1

    sibling = z * 2 + other

    def z_peer(d):
        return lax.rem(z + d, nz) * 2 + core

    def g_peer(d):
        return lax.rem(g + d + n_group, n_group)

    def span(c):
        return pl.ds(c * cols, cols)

    loads = {}

    def load(name, src, dst):
        copy = pltpu.make_async_copy(src, dst, load_sem.at[len(loads)])
        copy.start()
        loads[name] = copy

    load("num0", num_hbm.at[0, :, span(0)], cur.at[0])
    load("x0", x_hbm.at[0], x.at[0])
    for c in range(1, chunks):
        load(f"num{c}", num_hbm.at[0, :, span(c)], cur.at[c])
    for s in range(steps):
        load(f"tgt{s}", tgt_hbm.at[s], tgt.at[s])
    for c in range(chunks):
        load(f"mom{c}", mom_hbm.at[0, :, span(c)], vel.at[c])
        load(f"rec{c}", rec_hbm.at[0, :, span(c)], arr.at[c])
    for s in range(1, steps):
        load(f"x{s}", x_hbm.at[s], x.at[s])

    barrier = pltpu.get_barrier_semaphore()
    offsets = []
    for s in range(steps):
        for d in (2**s, -(2**s)):
            if d % n_group and d % n_group not in offsets:
                offsets.append(d % n_group)
    for d in offsets:
        pl.semaphore_signal(barrier, inc=1, device_id={"group": g_peer(d)}, device_id_type=MESH)
    for d in range(1, nz):
        pl.semaphore_signal(barrier, inc=1, device_id={"mp": z_peer(d)}, device_id_type=MESH)
    pl.semaphore_signal(barrier, inc=1, device_id={"mp": sibling}, device_id_type=MESH)
    pl.semaphore_wait(barrier, len(offsets) + nz)

    keep = [mix_ref[0, s].astype(f32) / 8.0 for s in range(steps)]
    weights = [pw_ref[0], keep[0] * pw_ref[0] + rw_ref[0]]
    w_copies = []
    for s in range(steps):
        outgoing_weight = jnp.full(wsend.shape[1:], (1.0 - keep[s]) * weights[s], f32)
        wsend[s] = outgoing_weight.astype(bf16).astype(f32)
        copy = pltpu.make_async_remote_copy(
            wsend.at[s], wrecv.at[s], w_send.at[s], w_recv.at[s],
            device_id={"group": g_peer(2**s)}, device_id_type=MESH,
        )
        copy.start()
        w_copies.append(copy)

    sends, stores = [], []
    sib_c, rs_c, ag_c, fwd_c, msg_c = {}, {}, {}, {}, {}

    def remote(src, dst, send, recv, where):
        copy = pltpu.make_async_remote_copy(src, dst, send, recv, device_id=where, device_id_type=MESH)
        copy.start()
        sends.append(copy)
        return copy

    def forward(j):
        s, c = divmod(j, chunks)
        if s == 0:
            loads[f"num{c}"].wait()
        if j == 0:
            loads["x0"].wait()
        sc[...] = (cur[c].astype(f32) / weights[s]).astype(bf16)
        half_z = nz // 2
        tile = half_z * 2 * own

        def body(i, _):
            lhs = x[s, pl.ds(pl.multiple_of(i * tile, tile), tile), :]
            product = jnp.dot(lhs, sc[...], preferred_element_type=f32) * row_scale
            part[j, pl.ds(i * half_z, half_z)] = product.astype(bf16).reshape(half_z, 2, own, cols)
            return 0

        lax.fori_loop(0, 2, body, 0)
        sib_c[j] = remote(part.at[j, :, other], sib.at[j], sib_send.at[j], sib_recv.at[j], {"mp": sibling})

    def pair_sum(j):
        sib_c[j].wait_recv()
        for k in range(nz):
            pair[j, k] = (part[j, k, core].astype(f32) + sib[j, k].astype(f32)).astype(bf16)
        for d in range(1, nz):
            rs_c[j, d] = remote(
                pair.at[j, lax.rem(z + d, nz)], peers.at[j, d - 1],
                rs_send.at[j, d - 1], rs_recv.at[j, d - 1], {"mp": z_peer(d)},
            )

    def value(j):
        s, c = divmod(j, chunks)
        total = pair[j, z].astype(f32)
        for d in range(1, nz):
            rs_c[j, d].wait_recv()
            total += peers[j, d - 1].astype(f32)
        values = total.astype(bf16)
        columns = slice(c * cols, (c + 1) * cols)
        val[s, :, columns] = values
        if c == 0:
            loads[f"tgt{s}"].wait()
        res[j, z, core] = (values.astype(f32) - tgt[s, :, columns].astype(f32)).astype(bf16)
        for d in range(1, nz):
            ag_c[j, d] = remote(
                res.at[j, z, core], res.at[j, z, core],
                ag_send.at[j, d - 1], ag_recv.at[j, d - 1], {"mp": z_peer(d)},
            )
        if c == chunks - 1:
            store = pltpu.make_async_copy(val.at[s], vr_hbm.at[s], store_sem.at[s])
            store.start()
            stores.append(store)

    def pass_on(j):
        for d in range(1, nz):
            source = lax.rem(z - d + nz, nz)
            pltpu.make_async_remote_copy(
                res.at[j, z, core], res.at[j, source, core],
                ag_send.at[j, d - 1], ag_recv.at[j, d - 1],
                device_id={"mp": z_peer(d)}, device_id_type=MESH,
            ).wait_recv()
        remote(res.at[j, :, core], res.at[j, :, core], fwd_send.at[j], fwd_recv.at[j], {"mp": sibling})

    def update(j):
        s, c = divmod(j, chunks)
        pltpu.make_async_remote_copy(
            res.at[j, :, core], res.at[j, :, other], fwd_send.at[j], fwd_recv.at[j],
            device_id={"mp": sibling}, device_id_type=MESH,
        ).wait_recv()
        if s == 0:
            loads[f"mom{c}"].wait()
            loads[f"rec{c}"].wait()
        else:
            landing(j - chunks).wait_recv()
        tile = min(256, width)

        def body(i, _):
            at = pl.ds(pl.multiple_of(i * tile, tile), tile)
            gradient = jnp.dot(
                xt[s, at, :], res[j].reshape(rows, cols), preferred_element_type=f32
            ) * grad_scale
            velocity = momentum_decay * vel[c, at, :] + gradient
            if s < steps - 1:
                vel[c, at, :] = velocity
            half_step = cur[c, at, :].astype(f32) - step_size * velocity
            out[j, at, :] = ((1.0 - keep[s]) * half_step).astype(bf16)
            landed = arr[c, at, :] if s == 0 else arr[chunks + c, at, :]
            cur[c, at, :] = (keep[s] * half_step + landed.astype(f32)).astype(bf16)
            return 0

        lax.fori_loop(0, width // tile, body, 0)
        if s == 0 and relayed(c):
            msg_c[j] = remote(
                out.at[j], arr.at[chunks + c + odd * chunks], msg_send.at[j],
                msg_recv.at[j + odd * jobs], {"group": g_peer(1 + odd)},
            )
        else:
            msg_c[j] = remote(
                out.at[j], arr.at[chunks + c if s == 0 else 3 * chunks + c],
                msg_send.at[j], msg_recv.at[j], {"group": g_peer(2**s)},
            )
        if s == steps - 1:
            store = pltpu.make_async_copy(cur.at[c], fnum_hbm.at[0, :, span(c)], store_sem.at[steps + c])
            store.start()
            stores.append(store)

    def landing(j):
        s, c = divmod(j, chunks)
        return pltpu.make_async_remote_copy(
            out.at[j], arr.at[chunks + c if s == 0 else 3 * chunks + c],
            msg_send.at[j], msg_recv.at[j],
            device_id={"group": g_peer(2**s)}, device_id_type=MESH,
        )

    def relay_copy(c):
        return pltpu.make_async_remote_copy(
            arr.at[2 * chunks + c], arr.at[chunks + c], relay_send.at[c], msg_recv.at[c],
            device_id={"group": g_peer(-1)}, device_id_type=MESH,
        )

    def relay(c):
        @pl.when(odd == 1)
        def _():
            pltpu.make_async_remote_copy(
                out.at[c], arr.at[2 * chunks + c], msg_send.at[c], msg_recv.at[c + jobs],
                device_id={"group": g_peer(2)}, device_id_type=MESH,
            ).wait_recv()
            relay_copy(c).start()

    def transpose(s, i, pieces):
        if s > 0 and i == 0:
            loads[f"x{s}"].wait()
        tile = width // pieces
        xt[s, i * tile:(i + 1) * tile, :] = x[s, :, i * tile:(i + 1) * tile].T

    stages = ((update, 5), (pass_on, 4), (value, 2), (pair_sum, 1), (forward, 0))
    depth = stages[0][1]
    first, second = list(range(chunks)), list(range(chunks, jobs))
    order = first[:depth]
    first = first[depth:]
    while second:
        order.append(second.pop(0))
        if first:
            order.append(first.pop(0))
    place = {j: i for i, j in enumerate(order)}
    for tick in range(jobs + depth):
        for stage, delay in stages:
            if 0 <= tick - delay < jobs:
                stage(order[tick - delay])
        for c in range(chunks):
            if relayed(c) and tick == place[c] + depth + 3:
                relay(c)
        for s in range(steps):
            if 0 <= tick - s * chunks // 2 < 4:
                transpose(s, tick - s * chunks // 2, 4)

    for copy in w_copies:
        copy.wait()
    fw_ref[...] = keep[1] * weights[1] + wrecv[0]
    frw_ref[...] = wrecv[1]
    for c in range(chunks):
        landing((steps - 1) * chunks + c).wait_recv()
        store = pltpu.make_async_copy(
            arr.at[3 * chunks + c], frec_hbm.at[0, :, span(c)], store_sem.at[steps + chunks + c]
        )
        store.start()
        stores.append(store)
    for copy in sends:
        copy.wait_send()
    for c in range(chunks):
        if relayed(c):
            @pl.when(odd == 1)
            def _():
                relay_copy(c).wait_send()
    for store in stores:
        store.wait()


def finish(fnum, frec, vr, fw, frw, fnum_out, fw_out, frec_out, frw_out, vr_out, hold, vr_hold, load_sem, store_sem):
    moves = []
    pieces, tile = hold.shape[1], hold.shape[2]
    for i, (src, dst) in enumerate(((fnum, fnum_out), (frec, frec_out))):
        for p in range(pieces):
            at = pl.ds(p * tile, tile)
            moves.append((src.at[0, at], hold.at[i, p], dst.at[0, at]))
    moves.append((vr, vr_hold, vr_out))
    loads, stores = [], []
    for i, (src, via, dst) in enumerate(moves):
        loads.append(pltpu.make_async_copy(src, via, load_sem.at[i]))
        stores.append(pltpu.make_async_copy(via, dst, store_sem.at[i]))
        loads[-1].start()
    fw_out[0] = fw[0, 0]
    frw_out[0] = frw[0, 0]
    for load, store in zip(loads, stores):
        load.wait()
        store.start()
    for store in stores:
        store.wait()


def local(inputs, targets, numerator, momentum, received, push_weight, received_weight, mix_share):
    steps, rows, width = inputs.shape
    own, kv = targets.shape[1], targets.shape[2]
    n_group, n_mp = lax.axis_size("group"), lax.axis_size("mp")
    chunks = 8
    cols = kv // chunks
    jobs = steps * chunks
    nz = n_mp // 2
    pieces = 4
    any_space = pl.BlockSpec(memory_space=pl.ANY)
    smem = pl.BlockSpec(memory_space=pltpu.SMEM)
    vmem = pl.BlockSpec(memory_space=pltpu.VMEM)
    dma = pltpu.SemaphoreType.DMA
    fnum, frec, vr, fw, frw = pl.pallas_call(
        functools.partial(kernel, n_group, n_mp, chunks, steps),
        out_shape=(
            jax.ShapeDtypeStruct(numerator.shape, bf16),
            jax.ShapeDtypeStruct(numerator.shape, bf16),
            jax.ShapeDtypeStruct(targets.shape, bf16),
            jax.ShapeDtypeStruct((8, 128), f32),
            jax.ShapeDtypeStruct((8, 128), f32),
        ),
        in_specs=[smem] * 3 + [any_space] * 5,
        out_specs=(any_space, any_space, any_space, vmem, vmem),
        scratch_shapes=[
            pltpu.VMEM((steps, rows, width), bf16),
            pltpu.VMEM((steps, width, rows), bf16),
            pltpu.VMEM((chunks, width, cols), bf16),
            pltpu.VMEM((chunks, width, cols), f32),
            pltpu.VMEM((4 * chunks, width, cols), bf16),
            pltpu.VMEM((steps, own, kv), bf16),
            pltpu.VMEM((jobs, nz, 2, own, cols), bf16),
            pltpu.VMEM((jobs, nz, own, cols), bf16),
            pltpu.VMEM((jobs, nz, own, cols), bf16),
            pltpu.VMEM((jobs, nz - 1, own, cols), bf16),
            pltpu.VMEM((jobs, nz, 2, own, cols), bf16),
            pltpu.VMEM((jobs, width, cols), bf16),
            pltpu.VMEM((width, cols), bf16),
            pltpu.VMEM((steps, own, kv), bf16),
            pltpu.VMEM((steps, 8, 128), f32),
            pltpu.VMEM((steps, 8, 128), f32),
            dma((3 * chunks + 2 * steps,)),
            dma((jobs,)), dma((jobs,)),
            dma((jobs, nz - 1)), dma((jobs, nz - 1)),
            dma((jobs, nz - 1)), dma((jobs, nz - 1)),
            dma((jobs,)), dma((jobs,)),
            dma((jobs,)), dma((2 * jobs,)), dma((chunks,)),
            dma((steps,)), dma((steps,)),
            dma((steps + 2 * chunks,)),
        ],
        compiler_params=pltpu.CompilerParams(
            collective_id=0, has_side_effects=True, vmem_limit_bytes=58 * 1024 * 1024
        ),
    )(push_weight, received_weight, mix_share, inputs, targets, numerator, momentum, received)
    return pl.pallas_call(
        finish,
        out_shape=(
            jax.ShapeDtypeStruct(numerator.shape, bf16),
            jax.ShapeDtypeStruct(push_weight.shape, f32),
            jax.ShapeDtypeStruct(numerator.shape, bf16),
            jax.ShapeDtypeStruct(push_weight.shape, f32),
            jax.ShapeDtypeStruct(targets.shape, bf16),
        ),
        in_specs=[any_space, any_space, any_space, vmem, vmem],
        out_specs=(any_space, smem, any_space, smem, any_space),
        scratch_shapes=[
            pltpu.VMEM((2, pieces, width // pieces, kv), bf16),
            pltpu.VMEM(targets.shape, bf16),
            dma((2 * pieces + 1,)), dma((2 * pieces + 1,)),
        ],
        compiler_params=pltpu.CompilerParams(vmem_limit_bytes=58 * 1024 * 1024),
    )(fnum, frec, vr, fw, frw)


def solution(mesh):
    placed = (
        P(None, "group", "mp"),
        P(None, ("group", "mp"), None),
        P("group", "mp", None),
        P("group", "mp", None),
        P("group", "mp", None),
        P("group"),
        P("group"),
        P("group", None),
    )
    return jax.shard_map(
        local,
        mesh=mesh,
        in_specs=placed,
        out_specs=(
            P("group", "mp", None),
            P("group"),
            P("group", "mp", None),
            P("group"),
            P(None, ("group", "mp"), None),
        ),
        check_vma=False,
    )
```
